32 devices in a mesh: parts: 2 (over y), rows: 4 (over z), ex: 4 (over x, core).
Axes of the slice: x: 2, y: 2, z: 4, core: 2. Of those that a mesh axis runs over, the one named last changes fastest.
Arguments:
- hidden_acts: bfloat16 [1024, 512], P(('parts', 'ex'), 'rows'), parts along dimension 0, may hold values from -6 to 6
- cotangent: bfloat16 [1024, 4096], P(('parts', 'ex'), 'rows'), parts along dimension 0, may hold values from -0.796875 to 0.796875
- lengths: int32 [64], P('parts'), parts along dimension 0, may hold values from 1 to 64, 512 in all
- row_signs: int32 [512], P('rows'), may hold values from -1 to 1, as said below
- col_signs: int32 [4096], replicated, may hold values from -1 to 1, as said below
- feat_row: int32 [8192], replicated, may hold values from 0 to 511
- feat_col: int32 [8192], replicated, may hold values from 0 to 4095
- inverse_rows: bfloat16 [8192, 8192], P('rows'), as said below
Outputs:
- scores: bfloat16 [64, 8192], P(('parts', 'ex'), 'rows'), parts along dimension 0
The draws below stay inside these ranges and needn't reach their ends.
There are 2 independent parts, one for each index of `parts`. The reference program is written for one: setup_inputs(seed, part) draws one part's arguments, and reference() takes and returns one part's arrays. A program takes and returns all parts, laid end to end along the dimension named above; an argument that names none is the same for every part. Nothing has to cross between parts.
Inputs may be any that keep to these rules, and one draw needn't show every extreme that they name: `row_signs`: every entry is -1 or +1. `col_signs`: every entry is -1 or +1. `inverse_rows`: the whole matrix equals its transpose. The lengths sum to 512 and the largest equals 64.
All inputs are finite; a program needn't handle non-finite values.
Results may differ from the reference program's by a relative error of at most 0.0049.
Values may be sent and summed in bfloat16 or wider, within the bound.
No kernel may reach another device: no remote copies, remote signals or barrier semaphores. Data moves between devices by JAX's collectives and lax.ppermute only.
A program may use at most 128 MiB of HBM per device.

```python
import math
import jax
import jax.numpy as jnp
import numpy as np
from jax import lax

D = 4096
FFW_DEV = 128
FFW = 512
K = 8192
EXAMPLES = 32
TOKENS = 512
MOST = 64
N_ROWS = 4


def draw_row_signs(key, part):
    return (2 * jax.random.randint(key, (FFW,), 0, 2) - 1).astype(jnp.int32)


def draw_col_signs(key, part):
    return (2 * jax.random.randint(key, (D,), 0, 2) - 1).astype(jnp.int32)


def draw_inverse_rows(key, part):
    base = jax.random.normal(key, (K, K), jnp.float32)
    mixed = (base + base.T) / jnp.sqrt(2.0 * K)
    weight = 0.3
    return (jnp.eye(K, dtype=jnp.float32) + weight * mixed).astype(jnp.bfloat16)


def place_ends(values, stream_key, smallest, high):
    dims = values.shape
    spot = [jax.random.randint(jax.random.fold_in(stream_key, axis), (), 0, dims[axis]) for axis in range(len(dims))]
    values = values.at[tuple(spot)].set(smallest)
    longest = dims.index(max(dims))
    spot[longest] = (spot[longest] + 1) % dims[longest]
    return values.at[tuple(spot)].set(high)


def levels(key, extent, split, smallest, largest):
    level = 1.0
    for dim, shards_of in split:
        heights = jax.random.uniform(jax.random.fold_in(jax.random.fold_in(key, 6), dim), (shards_of,), jnp.float32, smallest / len(split), largest / len(split))
        level = level * jnp.repeat(jnp.exp(heights), extent[dim] // shards_of).reshape((-1,) + (1,) * (len(extent) - 1 - dim))
    return level


def split_up(number_of, total, most, lean):
    portions = [(1 << 20) // math.isqrt(standing ** lean) + 1 for standing in range(2, number_of + 1)]
    rest, counts = total - most - (number_of - 1), [1] * (number_of - 1)
    while rest > 0:
        free = [i for i in range(number_of - 1) if counts[i] < most]
        pool, left = sum([portions[i] for i in free]), rest
        for i in free:
            more = min(most - counts[i], max(1, left * portions[i] // pool), rest)
            counts[i] = counts[i] + more
            rest = rest - more
    return np.array([most] + counts)


def ragged_sizes(own_key, number_of, total, most, lean):
    if number_of == 2:
        one = jax.random.randint(own_key, (), max(1, total - most), min(most, total - 1) + 1)
        return jnp.stack([one, total - one])
    sizes = jnp.asarray(split_up(number_of, total, most, lean), jnp.int32)
    twos = (number_of - 1) // 2
    source_of, sink = sizes[1:1 + 2 * twos:2], sizes[2:2 + 2 * twos:2]
    room = jnp.minimum(source_of - 1, most - sink)
    shifted = jax.random.randint(jax.random.fold_in(own_key, 1), (twos,), 0, 1 << 20) % (room + 1)
    sizes = sizes.at[1:1 + 2 * twos:2].set(source_of - shifted).at[2:2 + 2 * twos:2].set(sink + shifted)
    return sizes[jax.random.permutation(jax.random.fold_in(own_key, 2), number_of)]


def normal_values(rng, shape, width, limit, pieces=(), kind=jnp.bfloat16):
    result = jax.random.normal(rng, shape, jnp.float32) * width
    if len(pieces) > 0:
        result = levels(rng, shape, pieces, -0.22, 0.18) * result
    return jnp.clip(result, min=-limit, max=limit).astype(kind)


def setup_inputs(seed: int = 0, part: int = 0) -> dict:
    key_of = jax.random.split(jax.random.key(seed), 9)
    part_keys = jax.random.split(jax.random.fold_in(key_of[8], part), 9)
    hidden_acts = normal_values(part_keys[0], (TOKENS, FFW), 1.0, 6.0, ((0, 4), (1, 4)))
    cotangent = normal_values(part_keys[1], (TOKENS, D), 0.1, 0.796875, ((0, 4), (1, 4)))
    lengths = ragged_sizes(part_keys[2], EXAMPLES, TOKENS, MOST, 2).astype(jnp.int32)
    row_signs = draw_row_signs(jax.random.fold_in(key_of[8], 71), part)
    col_signs = draw_col_signs(jax.random.fold_in(key_of[8], 71), part)
    feat_row = place_ends(jax.random.randint(key_of[5], (K,), 0, FFW), jax.random.fold_in(key_of[5], 1), 0, FFW - 1).astype(jnp.int32)
    feat_col = place_ends(jax.random.randint(key_of[6], (K,), 0, D), jax.random.fold_in(key_of[6], 1), 0, D - 1).astype(jnp.int32)
    inverse_rows = draw_inverse_rows(jax.random.fold_in(key_of[8], 71), part)
    return {"hidden_acts": hidden_acts, "cotangent": cotangent, "lengths": lengths, "row_signs": row_signs, "col_signs": col_signs, "feat_row": feat_row, "feat_col": feat_col, "inverse_rows": inverse_rows}


def hadamard(mat_size):
    indices = jnp.arange(mat_size, dtype=jnp.int32)
    common = indices[:, None] & indices[None, :]
    parity = jnp.zeros((mat_size, mat_size), jnp.int32)
    for bit_pos in range(max(mat_size.bit_length() - 1, 0)):
        parity = parity + (common >> bit_pos & 1)
    return (1 - 2 * (parity % 2)).astype(jnp.float32)

def kron_apply(values, outer_mat, inner_mat):
    tokens = values.shape[0]
    shaped = values.reshape(tokens, outer_mat.shape[0], inner_mat.shape[0])
    shaped = jnp.einsum('tri,ia->tra', shaped, inner_mat, precision=lax.Precision.HIGHEST)
    shaped = jnp.einsum('tra,rh->tha', shaped, outer_mat, precision=lax.Precision.HIGHEST)
    return shaped.reshape(tokens, -1)

def reference(hidden_acts, cotangent, lengths, row_signs, col_signs, feat_row, feat_col, inverse_rows):
    left_side = hidden_acts.astype(jnp.float32) * row_signs.astype(jnp.float32)[None, :]
    left_side = kron_apply(left_side, hadamard(N_ROWS), hadamard(FFW_DEV))
    inner_width = min(D, 128)
    right_side = cotangent.astype(jnp.float32) * col_signs.astype(jnp.float32)[None, :]
    right_side = kron_apply(right_side, hadamard(D // inner_width), hadamard(inner_width))
    ex_end = jnp.cumsum(lengths).astype(jnp.int32)
    positions = jnp.arange(TOKENS, dtype=jnp.int32)
    owner = lax.optimization_barrier(jnp.sum((positions[:, None] >= ex_end[None, :]).astype(jnp.int32), axis=1))
    member = (owner[:, None] == jnp.arange(EXAMPLES, dtype=jnp.int32)[None, :]).astype(jnp.float32)
    picked = jnp.take(left_side, feat_row, axis=1) * jnp.take(right_side, feat_col, axis=1)
    features = jnp.dot(member.T, picked, precision=lax.Precision.HIGHEST) * (1.0 / math.sqrt(FFW * D))
    features_low = features.astype(jnp.bfloat16)
    return jnp.dot(features_low, inverse_rows, preferred_element_type=jnp.float32).astype(jnp.bfloat16)
```

```python
import functools
import math

import jax
import jax.numpy as jnp
from jax import lax
from jax.experimental import pallas as pl
from jax.experimental.pallas import tpu as pltpu
from jax.sharding import PartitionSpec as P

f32 = jnp.float32
bf16 = jnp.bfloat16
contract_last = (((1,), (1,)), ((), ()))
vmem_bytes = 30 * 2**20


def swap(values, axis, mask):
    size = lax.axis_size(axis)
    return lax.ppermute(values, axis, [(rank, rank ^ mask) for rank in range(size)])


def bit_sign(index, bit_pos):
    return (1 - 2 * (index >> bit_pos & 1)).astype(f32)


def parity_sign(bits, bit_count):
    parity = bits & 1
    for bit_pos in range(1, bit_count):
        parity = parity ^ (bits >> bit_pos & 1)
    return (1 - 2 * parity).astype(f32)


def sign_columns(index, size):
    columns = index.shape[1]
    first = min(size, 16)
    row_id = lax.broadcasted_iota(jnp.int32, (first, columns), 0)
    first_bits = first.bit_length() - 1
    table = parity_sign(row_id & index, first_bits).astype(bf16)
    for bit_pos in range(first_bits, size.bit_length() - 1):
        table = jnp.concatenate([table, table * bit_sign(index, bit_pos).astype(bf16)], axis=0)
    return table


def index_row(ref, start, count):
    rows = [ref[pl.ds(start + step, 1), :] for step in range(count)]
    return jnp.concatenate(rows, axis=1)


def cot_products(values, index, block):
    size = values.shape[1]
    base_size = min(size, block)
    base = sign_columns(index, base_size)
    total = None
    for part in range(size // base_size):
        table = base
        if part > 0:
            sign = parity_sign((index // base_size) & part, (size // base_size).bit_length() - 1)
            table = base * sign.astype(bf16)
        piece = jnp.dot(
            values[:, part * base_size : (part + 1) * base_size], table, preferred_element_type=f32
        )
        total = piece if total is None else total + piece
    return total


def right_kernel(is_own, row_count, cot_ref, sign_ref, col_ref, *refs):
    out_ref = refs[-1]
    rank = lax.axis_index("rows")
    block_id = rank if is_own else rank ^ 1
    width = cot_ref.shape[1]
    model_sign = sign_ref[pl.ds(block_id, 1), :].astype(bf16)
    values = cot_ref[...] * model_sign
    lanes = col_ref.shape[1]
    half_rows = col_ref.shape[0] // 2
    first_row = (rank & 1) * half_rows
    columns = out_ref.shape[2]
    group = min(4, columns // lanes)
    row_bits = row_count.bit_length() - 1
    for step in range(half_rows // group):
        index = index_row(col_ref, first_row + step * group, group)
        local_index = index % width
        part = cot_products(values, local_index, 256)
        part = part * parity_sign((index // width) & block_id, row_bits)
        half = step * group * lanes // columns
        at = step * group * lanes % columns
        if not is_own:
            part = part + refs[0][half, :, at : at + group * lanes]
        out_ref[half, :, at : at + group * lanes] = part


def feature_kernel(flip, row_count, hidden_refs, right_ref, row_ref, len_ref, out_ref):
    rank = lax.axis_index("rows")
    ex_rank = lax.axis_index("ex")
    ex_count = lax.axis_size("ex")
    half = (ex_rank & 1) ^ flip
    tokens = right_ref.shape[1]
    width = hidden_refs[0].shape[1]
    examples = out_ref.shape[0]
    lanes = row_ref.shape[1]
    quarter_rows = row_ref.shape[0] // 4
    first_row = ((rank & 1) * 2 + half) * quarter_rows
    row_bits = row_count.bit_length() - 1
    own = examples // ex_count
    shape = (examples, examples)
    row_id = lax.broadcasted_iota(jnp.int32, shape, 0)
    example = ((row_id // own) ^ (ex_rank & ~1) ^ (ex_count - 2)) * own + row_id % own
    other = lax.broadcasted_iota(jnp.int32, shape, 1)
    counts = jnp.broadcast_to(len_ref[...], shape)
    ends = jnp.sum(jnp.where(other <= example, counts, 0), axis=1, keepdims=True)
    starts = jnp.sum(jnp.where(other < example, counts, 0), axis=1, keepdims=True)
    position = ex_rank * tokens + lax.broadcasted_iota(jnp.int32, (examples, tokens), 1)
    member = jnp.logical_and(position >= starts, position < ends).astype(f32).astype(bf16)
    group = min(4, quarter_rows)
    for step in range(quarter_rows // group):
        index = index_row(row_ref, first_row + step * group, group)
        base = sign_columns(index % width, width)
        high = index // width
        left = None
        offset = 0
        for ref in hidden_refs:
            blocks = ref.shape[0]
            for block in range(blocks):
                block_id = rank ^ (offset + block)
                table = base * parity_sign(high & block_id, row_bits).astype(bf16)
                piece = jnp.dot(ref[block], table, preferred_element_type=f32)
                left = piece if left is None else left + piece
            offset += blocks
        columns = slice(step * group * lanes, (step + 1) * group * lanes)
        product = left * right_ref[half, :, columns]
        high_part = product.astype(bf16)
        low_part = (product - high_part.astype(f32)).astype(bf16)
        out_ref[:, columns] = jnp.dot(member, high_part, preferred_element_type=f32) + jnp.dot(
            member, low_part, preferred_element_type=f32
        )


def score_kernel(is_own, low_ref, matrix_ref, *refs):
    if is_own:
        out_ref, held, sems = refs
    else:
        sum_ref, send_ref, keep_ref, held, sems = refs
    rank = lax.axis_index("rows")
    ex_rank = lax.axis_index("ex")
    depth = low_ref.shape[1]
    half = (rank & 1) if is_own else (rank & 1) ^ 1
    first = pl.multiple_of((half * 2 + (ex_rank & 1)) * depth, depth)
    pieces, rows = held.shape[0], held.shape[1]
    copies = []
    for piece in range(pieces):
        copy = pltpu.make_async_copy(
            matrix_ref.at[pl.ds(piece * rows, rows), pl.ds(first, depth)],
            held.at[piece],
            sems.at[piece],
        )
        copy.start()
        copies.append(copy)
    low = low_ref[...]
    own = low.shape[0] // 2
    for piece in range(pieces):
        copies[piece].wait()
        part = lax.dot_general(low, held[piece], contract_last, preferred_element_type=f32)
        columns = slice(piece * rows, (piece + 1) * rows)
        if is_own:
            out_ref[:, columns] = part
        else:
            part = part + sum_ref[:, columns]
            lower = (ex_rank & 1) == 0
            keep_ref[:, columns] = jnp.where(lower, part[:own], part[own:])
            send_ref[:, columns] = jnp.where(lower, part[own:], part[:own])


def local(hidden_acts, cotangent, lengths, row_signs, col_signs, feat_row, feat_col, inverse_rows):
    row_count = lax.axis_size("rows")
    ex_count = lax.axis_size("ex")
    tokens, width = hidden_acts.shape
    model_width = col_signs.shape[0]
    feature_count = feat_row.shape[0]
    example_count = lengths.shape[0]
    quarter = feature_count // 4
    own_examples = example_count // ex_count
    norm_scale = 1.0 / math.sqrt(width * row_count * model_width)
    whole = pl.BlockSpec(memory_space=pltpu.VMEM)
    params = pltpu.CompilerParams(vmem_limit_bytes=vmem_bytes)

    signed = hidden_acts * row_signs.astype(bf16)[None, :]
    hidden_parts = [signed[None]]
    near = swap(signed[None], "rows", 1)
    near_cot = swap(cotangent, "rows", 1)
    hidden_parts.append(near)
    step = 2
    while step < row_count:
        held = jnp.concatenate(hidden_parts, axis=0)
        hidden_parts = [held, swap(held, "rows", step)]
        step *= 2

    col_table = col_signs.reshape(row_count, model_width // row_count)
    col_index = feat_col.reshape(-1, 128)
    row_index = feat_row.reshape(-1, 128)
    right_shape = jax.ShapeDtypeStruct((2, tokens, quarter), f32)
    right = pl.pallas_call(
        functools.partial(right_kernel, True, row_count),
        out_shape=right_shape,
        in_specs=[whole] * 3,
        out_specs=whole,
        compiler_params=params,
    )(cotangent, col_table, col_index)
    right = pl.pallas_call(
        functools.partial(right_kernel, False, row_count),
        out_shape=right_shape,
        in_specs=[whole] * 4,
        out_specs=whole,
        compiler_params=params,
    )(near_cot, col_table, col_index, right)

    def features(flip):
        def kernel(*refs):
            feature_kernel(flip, row_count, refs[: len(hidden_parts)], *refs[len(hidden_parts) :])

        return pl.pallas_call(
            kernel,
            out_shape=jax.ShapeDtypeStruct((example_count, quarter), f32),
            in_specs=[whole] * (len(hidden_parts) + 3),
            out_specs=whole,
            compiler_params=params,
        )(*hidden_parts, right, row_index, lengths.reshape(1, example_count))

    total = swap(features(1), "ex", 1) + features(0)
    mask = ex_count // 2
    while mask > 1:
        half = total.shape[0] // 2
        total = total[half:] + swap(total[:half].astype(bf16), "ex", mask).astype(f32)
        mask //= 2
    step = 2
    while step < row_count:
        total = total + swap(total.astype(bf16), "rows", step).astype(f32)
        step *= 2
    low = (total * norm_scale).astype(bf16)
    near_low = swap(low, "rows", 1)

    out_rows = inverse_rows.shape[0]
    pieces = max(out_rows // 256, 1)
    scratch = [
        pltpu.VMEM((pieces, out_rows // pieces, quarter), bf16),
        pltpu.SemaphoreType.DMA((pieces,)),
    ]
    anywhere = pl.BlockSpec(memory_space=pl.ANY)
    part = pl.pallas_call(
        functools.partial(score_kernel, True),
        out_shape=jax.ShapeDtypeStruct((2 * own_examples, out_rows), f32),
        in_specs=[whole, anywhere],
        out_specs=whole,
        scratch_shapes=scratch,
        compiler_params=params,
    )(low, inverse_rows)
    own_shape = jax.ShapeDtypeStruct((own_examples, out_rows), f32)
    send, keep = pl.pallas_call(
        functools.partial(score_kernel, False),
        out_shape=(own_shape, own_shape),
        in_specs=[whole, anywhere, whole],
        out_specs=(whole, whole),
        scratch_shapes=scratch,
        compiler_params=params,
    )(near_low, inverse_rows, part)
    return (keep + swap(send, "ex", 1)).astype(bf16)


def solution(mesh):
    placed = (
        P(("parts", "ex"), "rows"),
        P(("parts", "ex"), "rows"),
        P("parts"),
        P("rows"),
        P(),
        P(),
        P(),
        P("rows", None),
    )
    return jax.shard_map(
        local, mesh=mesh, in_specs=placed, out_specs=P(("parts", "ex"), "rows"), check_vma=False
    )
```

```python
import functools
import math

import jax
import jax.numpy as jnp
from jax import lax
from jax.experimental import pallas as pl
from jax.experimental.pallas import tpu as pltpu
from jax.sharding import PartitionSpec as P

f32 = jnp.float32
bf16 = jnp.bfloat16
contract_last = (((1,), (1,)), ((), ()))
vmem_bytes = 14 * 2**20


def in_hbm(values):
    return pltpu.with_memory_space_constraint(values, pltpu.HBM)


def swap(values, axis, mask):
    size = lax.axis_size(axis)
    return lax.ppermute(values, axis, [(rank, rank ^ mask) for rank in range(size)])


def bit_sign(index, bit_pos):
    return (1 - 2 * (index >> bit_pos & 1)).astype(f32)


def parity_sign(bits, bit_count):
    parity = bits & 1
    for bit_pos in range(1, bit_count):
        parity = parity ^ (bits >> bit_pos & 1)
    return (1 - 2 * parity).astype(f32)


def sign_columns(index, size):
    columns = index.shape[1]
    first = min(size, 16)
    row_id = lax.broadcasted_iota(jnp.int32, (first, columns), 0)
    first_bits = first.bit_length() - 1
    table = parity_sign(row_id & index, first_bits).astype(bf16)
    for bit_pos in range(first_bits, size.bit_length() - 1):
        table = jnp.concatenate([table, table * bit_sign(index, bit_pos).astype(bf16)], axis=0)
    return table


def index_row(ref, start, count):
    rows = [ref[pl.ds(start + step, 1), :] for step in range(count)]
    return jnp.concatenate(rows, axis=1)


def cot_products(values, index, block):
    size = values.shape[1]
    base_size = min(size, block)
    base = sign_columns(index, base_size)
    total = None
    for part in range(size // base_size):
        table = base
        if part > 0:
            sign = parity_sign((index // base_size) & part, (size // base_size).bit_length() - 1)
            table = base * sign.astype(bf16)
        piece = jnp.dot(
            values[:, part * base_size : (part + 1) * base_size], table, preferred_element_type=f32
        )
        total = piece if total is None else total + piece
    return total


def right_block(values, col_ref, rank, block_id, row_count, store):
    width = values.shape[1]
    lanes = col_ref.shape[1]
    half_rows = col_ref.shape[0] // 2
    first_row = (rank & 1) * half_rows
    group = min(4, half_rows // 2)
    row_bits = row_count.bit_length() - 1
    for step in range(half_rows // group):
        index = index_row(col_ref, first_row + step * group, group)
        part = cot_products(values, index % width, 256)
        part = part * parity_sign((index // width) & block_id, row_bits)
        half = step * group // (half_rows // 2)
        at = step * group * lanes % (half_rows // 2 * lanes)
        store(half, slice(at, at + group * lanes), part)


def block_signs(sign_ref, block_id, width):
    rows = width // sign_ref.shape[1]
    return index_row(sign_ref, block_id * rows, rows).astype(bf16)


def matrix_slice(matrix_ref, is_own, depth):
    half = (lax.axis_index("rows") & 1) ^ (0 if is_own else 1)
    first = pl.multiple_of((half * 2 + (lax.axis_index("ex") & 1)) * depth, depth)
    return matrix_ref.at[:, pl.ds(first, depth)]


def sign_kernel(hidden_in, sign_in, out_ref, hidden_ref, sign_ref, sems):
    copies = [
        pltpu.make_async_copy(hidden_in, hidden_ref, sems.at[0]),
        pltpu.make_async_copy(sign_in, sign_ref, sems.at[1]),
    ]
    for copy in copies:
        copy.start()
    for copy in copies:
        copy.wait()
    out_ref[0] = hidden_ref[...] * sign_ref[...].astype(bf16)


def first_kernel(row_count, cot_in, sign_in, col_in, row_in, len_in, *refs):
    right_ref, near_sign_ref, col_ref, row_ref, len_ref, token_ref, cot_ref, sign_ref, sems = refs
    pairs = (
        (cot_in, cot_ref),
        (sign_in, sign_ref),
        (col_in, col_ref),
        (row_in, row_ref),
        (len_in, len_ref),
    )
    copies = [pltpu.make_async_copy(*pair, sems.at[at]) for at, pair in enumerate(pairs)]
    for copy in copies:
        copy.start()
    token_ref[...] = jnp.zeros_like(token_ref)
    for copy in copies:
        copy.wait()
    rank = lax.axis_index("rows")
    width = cot_ref.shape[1]
    near_sign_ref[...] = block_signs(sign_ref, rank ^ 1, width)
    values = cot_ref[...] * block_signs(sign_ref, rank, width)

    def store(half, columns, part):
        right_ref[half, :, columns] = part

    right_block(values, col_ref, rank, rank, row_count, store)


def right_kernel(row_count, cot_ref, sign_ref, col_ref, own_ref, out_ref):
    rank = lax.axis_index("rows")

    def store(half, columns, part):
        out_ref[half, :, columns] = own_ref[half, :, columns] + part

    right_block(cot_ref[...] * sign_ref[...], col_ref, rank, rank ^ 1, row_count, store)


def feature_kernel(flip, row_count, masks, hidden_refs, right_ref, row_ref, len_ref, out_ref):
    rank = lax.axis_index("rows")
    ex_rank = lax.axis_index("ex")
    ex_count = lax.axis_size("ex")
    half = (ex_rank & 1) ^ flip
    tokens = right_ref.shape[1]
    width = hidden_refs[0].shape[2]
    examples = out_ref.shape[0]
    lanes = row_ref.shape[1]
    quarter_rows = row_ref.shape[0] // 4
    first_row = ((rank & 1) * 2 + half) * quarter_rows
    row_bits = row_count.bit_length() - 1
    own = examples // ex_count
    shape = (examples, examples)
    row_id = lax.broadcasted_iota(jnp.int32, shape, 0)
    example = ((row_id // own) ^ (ex_rank & ~1) ^ (ex_count - 2)) * own + row_id % own
    other = lax.broadcasted_iota(jnp.int32, shape, 1)
    counts = jnp.broadcast_to(len_ref[...], shape)
    ends = jnp.sum(jnp.where(other <= example, counts, 0), axis=1, keepdims=True)
    starts = jnp.sum(jnp.where(other < example, counts, 0), axis=1, keepdims=True)
    position = ex_rank * tokens + lax.broadcasted_iota(jnp.int32, (examples, tokens), 1)
    member = jnp.logical_and(position >= starts, position < ends).astype(f32).astype(bf16)
    blocks = []
    for ref in hidden_refs:
        for block in range(ref.shape[0]):
            blocks.append(ref[block])
    group = min(4, quarter_rows)
    for step in range(quarter_rows // group):
        index = index_row(row_ref, first_row + step * group, group)
        base = sign_columns(index % width, width)
        high = index // width
        left = None
        for mask, values in zip(masks, blocks):
            table = base * parity_sign(high & (rank ^ mask), row_bits).astype(bf16)
            piece = jnp.dot(values, table, preferred_element_type=f32)
            left = piece if left is None else left + piece
        columns = slice(step * group * lanes, (step + 1) * group * lanes)
        product = left * right_ref[half, :, columns]
        high_part = product.astype(bf16)
        low_part = (product - high_part.astype(f32)).astype(bf16)
        out_ref[:, columns] = jnp.dot(member, high_part, preferred_element_type=f32) + jnp.dot(
            member, low_part, preferred_element_type=f32
        )


def load_kernel(is_own, matrix_ref, after_ref, out_ref, token_ref, sem):
    copy = pltpu.make_async_copy(matrix_slice(matrix_ref, is_own, out_ref.shape[1]), out_ref, sem)
    copy.start()
    token_ref[...] = jnp.zeros_like(token_ref)
    copy.wait()


def add_kernel(scale, kept_ref, received_ref, *refs):
    total = kept_ref[...] + received_ref[...].astype(f32)
    if scale is not None:
        refs[-1][...] = (total * scale).astype(bf16)
    else:
        send_ref, total_ref = refs[-2:]
        send_ref[...] = total[: send_ref.shape[0]].astype(bf16)
        total_ref[...] = total[total.shape[0] - total_ref.shape[0] :]


def score_kernel(is_own, low_ref, matrix_ref, *refs):
    part = lax.dot_general(
        low_ref[...], matrix_ref[...], contract_last, preferred_element_type=f32
    )
    if is_own:
        refs[0][...] = part
    else:
        sum_ref, send_ref, keep_ref = refs
        part = part + sum_ref[...]
        own = part.shape[0] // 2
        lower = (lax.axis_index("ex") & 1) == 0
        keep_ref[...] = jnp.where(lower, part[:own], part[own:])
        send_ref[...] = jnp.where(lower, part[own:], part[:own])


def local(hidden_acts, cotangent, lengths, row_signs, col_signs, feat_row, feat_col, inverse_rows):
    row_count = lax.axis_size("rows")
    ex_count = lax.axis_size("ex")
    tokens, width = hidden_acts.shape
    model_width = col_signs.shape[0]
    feature_count = feat_row.shape[0]
    example_count = lengths.shape[0]
    quarter = feature_count // 4
    own_examples = example_count // ex_count
    norm_scale = 1.0 / math.sqrt(width * row_count * model_width)
    whole = pl.BlockSpec(memory_space=pltpu.VMEM)
    params = pltpu.CompilerParams(vmem_limit_bytes=vmem_bytes)

    anywhere = pl.BlockSpec(memory_space=pltpu.HBM)
    out_rows = inverse_rows.shape[0]

    near_cot = swap(cotangent, "rows", 1)
    signed = pl.pallas_call(
        sign_kernel,
        out_shape=pltpu.VMEM((1, tokens, width), bf16),
        in_specs=[anywhere] * 2,
        out_specs=whole,
        scratch_shapes=[
            pltpu.VMEM((tokens, width), bf16),
            pltpu.VMEM((1, width), jnp.int32),
            pltpu.SemaphoreType.DMA((2,)),
        ],
        compiler_params=params,
    )(in_hbm(hidden_acts), in_hbm(row_signs.reshape(1, -1)))
    held = signed
    masks = [0]
    step = 2
    while step < row_count:
        held = jnp.concatenate([held, swap(held, "rows", step)], axis=0)
        masks += [mask | step for mask in masks]
        step *= 2
    masks += [mask | 1 for mask in masks]

    cot_width = cotangent.shape[1]
    right_shape = pltpu.VMEM((2, tokens, quarter), f32)
    lanes = min(128, cot_width)
    right, near_signs, col_index, row_index, counts, token = pl.pallas_call(
        functools.partial(first_kernel, row_count),
        out_shape=(
            right_shape,
            pltpu.VMEM((1, cot_width), bf16),
            pltpu.VMEM((feature_count // 128, 128), jnp.int32),
            pltpu.VMEM((feature_count // 128, 128), jnp.int32),
            pltpu.VMEM((1, example_count), jnp.int32),
            pltpu.VMEM((1, 1, 128), bf16),
        ),
        in_specs=[anywhere] * 5,
        out_specs=(whole,) * 6,
        scratch_shapes=[
            pltpu.VMEM(cotangent.shape, bf16),
            pltpu.VMEM((model_width // lanes, lanes), jnp.int32),
            pltpu.SemaphoreType.DMA((5,)),
        ],
        compiler_params=params,
    )(
        in_hbm(cotangent),
        in_hbm(col_signs.reshape(-1, lanes)),
        in_hbm(feat_col.reshape(-1, 128)),
        in_hbm(feat_row.reshape(-1, 128)),
        in_hbm(lengths.reshape(1, -1)),
    )
    held = held + token[:, :, :1]
    hidden_parts = (held, swap(held, "rows", 1))
    right = pl.pallas_call(
        functools.partial(right_kernel, row_count),
        out_shape=right_shape,
        in_specs=[whole] * 4,
        out_specs=whole,
        compiler_params=params,
    )(near_cot, near_signs, col_index, right)

    def features(flip):
        def kernel(*refs):
            feature_kernel(flip, row_count, masks, refs[:2], *refs[2:])

        return pl.pallas_call(
            kernel,
            out_shape=jax.ShapeDtypeStruct((example_count, quarter), f32),
            in_specs=[whole] * 5,
            out_specs=whole,
            compiler_params=params,
        )(*hidden_parts, right, row_index, counts)

    def load(is_own, after):
        return pl.pallas_call(
            functools.partial(load_kernel, is_own),
            out_shape=(pltpu.VMEM((out_rows, quarter), bf16), pltpu.VMEM((8, 128), f32)),
            in_specs=[anywhere, whole],
            out_specs=(whole, whole),
            scratch_shapes=[pltpu.SemaphoreType.DMA],
            compiler_params=params,
        )(in_hbm(inverse_rows), after)

    def add_up(kept, received, send_count, token, scale=None):
        count = received.shape[0]
        out_shape = [pltpu.VMEM((send_count, quarter), bf16)]
        if scale is None:
            out_shape.append(pltpu.VMEM((count - send_count % count, quarter), f32))
        return pl.pallas_call(
            functools.partial(add_kernel, scale),
            out_shape=out_shape,
            in_specs=[whole] * (2 + (token is not None)),
            out_specs=[whole] * len(out_shape),
            compiler_params=params,
        )(kept, received, *([] if token is None else [token]))

    ex_masks = [1 << bit for bit in range(1, ex_count.bit_length() - 1)][::-1]
    row_masks = [1 << bit for bit in range(1, row_count.bit_length() - 1)]
    received = swap(features(1), "ex", 1)
    total = features(0)
    matrices, token = [], None
    hops = [("ex", mask) for mask in ex_masks] + [("rows", mask) for mask in row_masks]
    for axis, mask in hops:
        count = received.shape[0]
        send, total = add_up(total, received, count // 2 if axis == "ex" else count, token)
        token = None
        if len(matrices) < 2:
            matrix, token = load(len(matrices) == 0, send)
            matrices.append(matrix)
        received = swap(send, axis, mask)
    own_matrix, near_matrix = matrices
    (low,) = add_up(total, received, received.shape[0], token, norm_scale)
    near_low = swap(low, "rows", 1)

    part = pl.pallas_call(
        functools.partial(score_kernel, True),
        out_shape=jax.ShapeDtypeStruct((2 * own_examples, out_rows), f32),
        in_specs=[whole, whole],
        out_specs=whole,
        compiler_params=params,
    )(low, own_matrix)
    own_shape = jax.ShapeDtypeStruct((own_examples, out_rows), f32)
    send, keep = pl.pallas_call(
        functools.partial(score_kernel, False),
        out_shape=(own_shape, own_shape),
        in_specs=[whole, whole, whole],
        out_specs=(whole, whole),
        compiler_params=params,
    )(near_low, near_matrix, part)
    return (keep + swap(send, "ex", 1)).astype(bf16)


def solution(mesh):
    placed = (
        P(("parts", "ex"), "rows"),
        P(("parts", "ex"), "rows"),
        P("parts"),
        P("rows"),
        P(),
        P(),
        P(),
        P("rows", None),
    )
    return jax.shard_map(
        local, mesh=mesh, in_specs=placed, out_specs=P(("parts", "ex"), "rows"), check_vma=False
    )
```

```python
import functools
import math

import jax
import jax.numpy as jnp
from jax import lax
from jax.experimental import pallas as pl
from jax.experimental.pallas import tpu as pltpu
from jax.sharding import PartitionSpec as P

f32 = jnp.float32
bf16 = jnp.bfloat16
contract_last = (((1,), (1,)), ((), ()))
vmem_bytes = 14 * 2**20


def in_hbm(values):
    return pltpu.with_memory_space_constraint(values, pltpu.HBM)


def swap(values, axis, mask):
    size = lax.axis_size(axis)
    return lax.ppermute(values, axis, [(rank, rank ^ mask) for rank in range(size)])


def bit_sign(index, bit_pos):
    return (1 - 2 * (index >> bit_pos & 1)).astype(f32)


def parity_sign(bits, bit_count):
    parity = bits & 1
    for bit_pos in range(1, bit_count):
        parity = parity ^ (bits >> bit_pos & 1)
    return (1 - 2 * parity).astype(f32)


def sign_columns(index, size):
    columns = index.shape[1]
    first = min(size, 16)
    row_id = lax.broadcasted_iota(jnp.int32, (first, columns), 0)
    first_bits = first.bit_length() - 1
    table = parity_sign(row_id & index, first_bits).astype(bf16)
    for bit_pos in range(first_bits, size.bit_length() - 1):
        table = jnp.concatenate([table, table * bit_sign(index, bit_pos).astype(bf16)], axis=0)
    return table


def index_row(ref, start, count):
    rows = [ref[pl.ds(start + step, 1), :] for step in range(count)]
    return jnp.concatenate(rows, axis=1)


def cot_products(values, index, block):
    size = values.shape[1]
    base_size = min(size, block)
    base = sign_columns(index, base_size)
    total = None
    for part in range(size // base_size):
        table = base
        if part > 0:
            sign = parity_sign((index // base_size) & part, (size // base_size).bit_length() - 1)
            table = base * sign.astype(bf16)
        piece = jnp.dot(
            values[:, part * base_size : (part + 1) * base_size], table, preferred_element_type=f32
        )
        total = piece if total is None else total + piece
    return total


def right_block(values, col_ref, rank, block_id, row_count, store):
    width = values.shape[1]
    lanes = col_ref.shape[1]
    half_rows = col_ref.shape[0] // 2
    first_row = (rank & 1) * half_rows
    group = min(4, half_rows // 2)
    row_bits = row_count.bit_length() - 1
    for step in range(half_rows // group):
        index = index_row(col_ref, first_row + step * group, group)
        part = cot_products(values, index % width, 256)
        part = part * parity_sign((index // width) & block_id, row_bits)
        half = step * group // (half_rows // 2)
        at = step * group * lanes % (half_rows // 2 * lanes)
        store(half, slice(at, at + group * lanes), part)


def block_signs(sign_ref, block_id, width):
    rows = width // sign_ref.shape[1]
    return index_row(sign_ref, block_id * rows, rows).astype(bf16)


def matrix_chunk(matrix_ref, chunk, shape):
    rows, depth = shape
    half = (lax.axis_index("rows") & 1) ^ (chunk // 2)
    first = pl.multiple_of((half * 2 + (lax.axis_index("ex") & 1)) * depth, depth)
    return matrix_ref.at[pl.ds(chunk % 2 * rows, rows), pl.ds(first, depth)]


def sign_kernel(hidden_in, sign_in, out_ref, hidden_ref, sign_ref, sems):
    copies = [
        pltpu.make_async_copy(hidden_in, hidden_ref, sems.at[0]),
        pltpu.make_async_copy(sign_in, sign_ref, sems.at[1]),
    ]
    for copy in copies:
        copy.start()
    for copy in copies:
        copy.wait()
    out_ref[0] = hidden_ref[...] * sign_ref[...].astype(bf16)


def own_kernel(row_count, *refs):
    (cot_in, sign_in, col_in, row_in, len_in, matrix_ref), refs = refs[:6], refs[6:]
    right_ref, near_sign_ref, table_ref, member_ref, held_ref, col_ref, row_ref = refs[:7]
    cot_ref, sign_ref, len_ref, sems = refs[7:]
    pairs = (
        (cot_in, cot_ref),
        (sign_in, sign_ref),
        (col_in, col_ref),
        (row_in, row_ref),
        (len_in, len_ref),
        (matrix_chunk(matrix_ref, 0, held_ref.shape), held_ref),
    )
    copies = [pltpu.make_async_copy(*pair, sems.at[at]) for at, pair in enumerate(pairs)]
    for copy in copies:
        copy.start()
    for copy in copies[:-1]:
        copy.wait()
    rank = lax.axis_index("rows")
    width = cot_ref.shape[1]
    near_sign_ref[...] = block_signs(sign_ref, rank ^ 1, width)

    def store(half, columns, part):
        right_ref[half, :, columns] = part

    values = cot_ref[...] * block_signs(sign_ref, rank, width)
    right_block(values, col_ref, rank, rank, row_count, store)
    tables(row_ref, len_ref, table_ref, member_ref)
    copies[-1].wait()


def tables(row_ref, len_ref, table_ref, member_ref):
    rank = lax.axis_index("rows")
    lanes = row_ref.shape[1]
    quarter_rows = row_ref.shape[0] // 4
    first_row = (rank & 1) * 2 * quarter_rows
    width = table_ref.shape[1]
    group = min(4, quarter_rows)
    for step in range(2 * quarter_rows // group):
        index = index_row(row_ref, first_row + step * group, group)
        at = step * group % quarter_rows * lanes
        table_ref[step * group // quarter_rows, :, at : at + group * lanes] = sign_columns(
            index % width, width
        )
    examples, tokens = member_ref.shape
    ex_rank = lax.axis_index("ex")
    ex_count = lax.axis_size("ex")
    own = examples // ex_count
    shape = (examples, examples)
    row_id = lax.broadcasted_iota(jnp.int32, shape, 0)
    example = ((row_id // own) ^ (ex_rank & ~1) ^ (ex_count - 2)) * own + row_id % own
    other = lax.broadcasted_iota(jnp.int32, shape, 1)
    counts = jnp.broadcast_to(len_ref[...], shape)
    ends = jnp.sum(jnp.where(other <= example, counts, 0), axis=1, keepdims=True)
    starts = jnp.sum(jnp.where(other < example, counts, 0), axis=1, keepdims=True)
    position = ex_rank * tokens + lax.broadcasted_iota(jnp.int32, (examples, tokens), 1)
    inside = jnp.logical_and(position >= starts, position < ends)
    member_ref[...] = inside.astype(f32).astype(bf16)


def right_kernel(row_count, cot_ref, sign_ref, col_ref, own_ref, out_ref):
    rank = lax.axis_index("rows")

    def store(half, columns, part):
        out_ref[half, :, columns] = own_ref[half, :, columns] + part

    right_block(cot_ref[...] * sign_ref[...], col_ref, rank, rank ^ 1, row_count, store)


def feature_kernel(flip, row_count, masks, hidden_refs, right_ref, row_ref, table_ref, member_ref, out_ref):
    rank = lax.axis_index("rows")
    half = (lax.axis_index("ex") & 1) ^ flip
    width = table_ref.shape[1]
    lanes = row_ref.shape[1]
    quarter_rows = row_ref.shape[0] // 4
    first_row = ((rank & 1) * 2 + half) * quarter_rows
    row_bits = row_count.bit_length() - 1
    blocks = []
    for ref in hidden_refs:
        for block in range(ref.shape[0]):
            blocks.append(ref[block])
    member = member_ref[...]
    group = min(4, quarter_rows)
    for step in range(quarter_rows // group):
        columns = slice(step * group * lanes, (step + 1) * group * lanes)
        index = index_row(row_ref, first_row + step * group, group)
        base = table_ref[half, :, columns]
        high = index // width
        left = None
        for first in range(0, len(masks), 4):
            table = [
                base * parity_sign(high & (rank ^ mask), row_bits).astype(bf16)
                for mask in masks[first : first + 4]
            ]
            piece = jnp.dot(
                jnp.concatenate(blocks[first : first + 4], axis=1),
                jnp.concatenate(table, axis=0),
                preferred_element_type=f32,
            )
            left = piece if left is None else left + piece
        product = left * right_ref[half, :, columns]
        high_part = product.astype(bf16)
        low_part = (product - high_part.astype(f32)).astype(bf16)
        out_ref[:, columns] = jnp.dot(member, high_part, preferred_element_type=f32) + jnp.dot(
            member, low_part, preferred_element_type=f32
        )


def load_kernel(chunk, matrix_ref, after_ref, out_ref, token_ref, sem):
    copy = pltpu.make_async_copy(matrix_chunk(matrix_ref, chunk, out_ref.shape), out_ref, sem)
    copy.start()
    token_ref[...] = jnp.zeros_like(token_ref)
    copy.wait()


def add_kernel(scale, kept_ref, received_ref, *refs):
    total = kept_ref[...] + received_ref[...].astype(f32)
    if scale is not None:
        refs[-1][...] = (total * scale).astype(bf16)
    else:
        send_ref, total_ref = refs[-2:]
        send_ref[...] = total[: send_ref.shape[0]].astype(bf16)
        total_ref[...] = total[total.shape[0] - total_ref.shape[0] :]


def own_score_kernel(low_ref, lower_ref, upper_ref, matrix_ref, out_ref, held_ref, sem):
    copy = pltpu.make_async_copy(matrix_chunk(matrix_ref, 3, held_ref.shape), held_ref, sem)
    copy.start()

    @pl.when(lax.axis_index("rows") >= 0)
    def _():
        rows = held_ref.shape[0]
        low = low_ref[...]
        for at, ref in enumerate((lower_ref, upper_ref)):
            out_ref[:, at * rows : (at + 1) * rows] = lax.dot_general(
                low, ref[...], contract_last, preferred_element_type=f32
            )

    copy.wait()


def near_score_kernel(low_ref, lower_ref, upper_ref, sum_ref, send_ref, keep_ref):
    rows = lower_ref.shape[0]
    low = low_ref[...]
    own = low.shape[0] // 2
    lower = (lax.axis_index("ex") & 1) == 0
    for at, ref in enumerate((lower_ref, upper_ref)):
        columns = slice(at * rows, (at + 1) * rows)
        part = lax.dot_general(low, ref[...], contract_last, preferred_element_type=f32)
        part = part + sum_ref[:, columns]
        keep_ref[:, columns] = jnp.where(lower, part[:own], part[own:])
        send_ref[:, columns] = jnp.where(lower, part[own:], part[:own])


def local(hidden_acts, cotangent, lengths, row_signs, col_signs, feat_row, feat_col, inverse_rows):
    row_count = lax.axis_size("rows")
    ex_count = lax.axis_size("ex")
    tokens, width = hidden_acts.shape
    model_width = col_signs.shape[0]
    feature_count = feat_row.shape[0]
    example_count = lengths.shape[0]
    quarter = feature_count // 4
    own_examples = example_count // ex_count
    norm_scale = 1.0 / math.sqrt(width * row_count * model_width)
    whole = pl.BlockSpec(memory_space=pltpu.VMEM)
    params = pltpu.CompilerParams(vmem_limit_bytes=vmem_bytes)

    anywhere = pl.BlockSpec(memory_space=pltpu.HBM)
    out_rows = inverse_rows.shape[0]

    chunk = (out_rows // 2, quarter)
    table_shape = (feature_count // 128, 128)

    near_cot = swap(cotangent, "rows", 1)
    signed = pl.pallas_call(
        sign_kernel,
        out_shape=pltpu.VMEM((1, tokens, width), bf16),
        in_specs=[anywhere] * 2,
        out_specs=whole,
        scratch_shapes=[
            pltpu.VMEM((tokens, width), bf16),
            pltpu.VMEM((1, width), jnp.int32),
            pltpu.SemaphoreType.DMA((2,)),
        ],
        compiler_params=params,
    )(in_hbm(hidden_acts), in_hbm(row_signs.reshape(1, -1)))
    group = min(row_count, 4)
    hidden_parts = [signed] + [swap(signed, "rows", mask) for mask in range(1, group)]
    masks = list(range(group))
    step = group
    while step < row_count:
        held = jnp.concatenate(hidden_parts, axis=0)
        hidden_parts = [held, swap(held, "rows", step)]
        masks += [mask | step for mask in masks]
        step *= 2
    parts = len(hidden_parts)

    cot_width = cotangent.shape[1]
    lanes = min(128, cot_width)
    right_shape = pltpu.VMEM((2, tokens, quarter), f32)
    right, near_signs, hidden_table, member, matrix_0, col_index, row_index = pl.pallas_call(
        functools.partial(own_kernel, row_count),
        out_shape=(
            right_shape,
            pltpu.VMEM((1, cot_width), bf16),
            pltpu.VMEM((2, width, quarter), bf16),
            pltpu.VMEM((example_count, tokens), bf16),
            pltpu.VMEM(chunk, bf16),
            pltpu.VMEM(table_shape, jnp.int32),
            pltpu.VMEM(table_shape, jnp.int32),
        ),
        in_specs=[anywhere] * 6,
        out_specs=(whole,) * 7,
        scratch_shapes=[
            pltpu.VMEM(cotangent.shape, bf16),
            pltpu.VMEM((model_width // lanes, lanes), jnp.int32),
            pltpu.VMEM((1, example_count), jnp.int32),
            pltpu.SemaphoreType.DMA((6,)),
        ],
        compiler_params=params,
    )(
        in_hbm(cotangent),
        in_hbm(col_signs.reshape(-1, lanes)),
        in_hbm(feat_col.reshape(-1, 128)),
        in_hbm(feat_row.reshape(-1, 128)),
        in_hbm(lengths.reshape(1, -1)),
        in_hbm(inverse_rows),
    )
    right = pl.pallas_call(
        functools.partial(right_kernel, row_count),
        out_shape=right_shape,
        in_specs=[whole] * 4,
        out_specs=whole,
        compiler_params=params,
    )(near_cot, near_signs, col_index, right)

    def features(flip):
        def kernel(*refs):
            feature_kernel(flip, row_count, masks, refs[:parts], *refs[parts:])

        return pl.pallas_call(
            kernel,
            out_shape=jax.ShapeDtypeStruct((example_count, quarter), f32),
            in_specs=[whole] * (parts + 4),
            out_specs=whole,
            compiler_params=params,
        )(*hidden_parts, right, row_index, hidden_table, member)

    def load(chunk_id, after):
        return pl.pallas_call(
            functools.partial(load_kernel, chunk_id),
            out_shape=(pltpu.VMEM(chunk, bf16), pltpu.VMEM((8, 128), f32)),
            in_specs=[anywhere, whole],
            out_specs=(whole, whole),
            scratch_shapes=[pltpu.SemaphoreType.DMA],
            compiler_params=params,
        )(in_hbm(inverse_rows), after)

    def add_up(kept, received, send_count, token, scale=None):
        count = received.shape[0]
        out_shape = [pltpu.VMEM((send_count, quarter), bf16)]
        if scale is None:
            out_shape.append(pltpu.VMEM((count - send_count % count, quarter), f32))
        return pl.pallas_call(
            functools.partial(add_kernel, scale),
            out_shape=out_shape,
            in_specs=[whole] * (2 + (token is not None)),
            out_specs=[whole] * len(out_shape),
            compiler_params=params,
        )(kept, received, *([] if token is None else [token]))

    ex_masks = [1 << bit for bit in range(1, ex_count.bit_length() - 1)][::-1]
    row_masks = [1 << bit for bit in range(1, row_count.bit_length() - 1)]
    received = swap(features(1), "ex", 1)
    total = features(0)
    matrices, token = [], None
    hops = [("ex", mask) for mask in ex_masks] + [("rows", mask) for mask in row_masks]
    for axis, mask in hops:
        count = received.shape[0]
        send, total = add_up(total, received, count // 2 if axis == "ex" else count, token)
        token = None
        if len(matrices) < 2:
            matrix, token = load(1 + len(matrices), send)
            matrices.append(matrix)
        received = swap(send, axis, mask)
    matrix_1, matrix_2 = matrices
    (low,) = add_up(total, received, received.shape[0], token, norm_scale)
    near_low = swap(low, "rows", 1)

    part, matrix_3 = pl.pallas_call(
        own_score_kernel,
        out_shape=(pltpu.VMEM((2 * own_examples, out_rows), f32), pltpu.VMEM(chunk, bf16)),
        in_specs=[whole] * 3 + [anywhere],
        out_specs=(whole, whole),
        scratch_shapes=[pltpu.SemaphoreType.DMA],
        compiler_params=params,
    )(low, matrix_0, matrix_1, in_hbm(inverse_rows))
    own_shape = pltpu.VMEM((own_examples, out_rows), f32)
    send, keep = pl.pallas_call(
        near_score_kernel,
        out_shape=(own_shape, own_shape),
        in_specs=[whole] * 4,
        out_specs=(whole, whole),
        compiler_params=params,
    )(near_low, matrix_2, matrix_3, part)
    return (keep + swap(send, "ex", 1)).astype(bf16)


def solution(mesh):
    placed = (
        P(("parts", "ex"), "rows"),
        P(("parts", "ex"), "rows"),
        P("parts"),
        P("rows"),
        P(),
        P(),
        P(),
        P("rows", None),
    )
    return jax.shard_map(
        local, mesh=mesh, in_specs=placed, out_specs=P(("parts", "ex"), "rows"), check_vma=False
    )
```

```python
import functools
import math

import jax
import jax.numpy as jnp
from jax import lax
from jax.experimental import pallas as pl
from jax.experimental.pallas import tpu as pltpu
from jax.sharding import PartitionSpec as P

f32 = jnp.float32
bf16 = jnp.bfloat16
contract_last = (((1,), (1,)), ((), ()))
vmem_bytes = 14 * 2**20


def in_hbm(values):
    return pltpu.with_memory_space_constraint(values, pltpu.HBM)


def swap(values, axis, mask):
    size = lax.axis_size(axis)
    return lax.ppermute(values, axis, [(rank, rank ^ mask) for rank in range(size)])


def bit_sign(index, bit_pos):
    return (1 - 2 * (index >> bit_pos & 1)).astype(f32)


def parity_sign(bits, bit_count):
    parity = bits & 1
    for bit_pos in range(1, bit_count):
        parity = parity ^ (bits >> bit_pos & 1)
    return (1 - 2 * parity).astype(f32)


def sign_columns(index, size):
    columns = index.shape[1]
    first = min(size, 16)
    row_id = lax.broadcasted_iota(jnp.int32, (first, columns), 0)
    first_bits = first.bit_length() - 1
    table = parity_sign(row_id & index, first_bits).astype(bf16)
    for bit_pos in range(first_bits, size.bit_length() - 1):
        table = jnp.concatenate([table, table * bit_sign(index, bit_pos).astype(bf16)], axis=0)
    return table


def index_row(ref, start, count):
    rows = [ref[pl.ds(start + step, 1), :] for step in range(count)]
    return jnp.concatenate(rows, axis=1)


def cot_products(values, index, block):
    size = values.shape[1]
    base_size = min(size, block)
    base = sign_columns(index, base_size)
    total = None
    for part in range(size // base_size):
        table = base
        if part > 0:
            sign = parity_sign((index // base_size) & part, (size // base_size).bit_length() - 1)
            table = base * sign.astype(bf16)
        piece = jnp.dot(
            values[:, part * base_size : (part + 1) * base_size], table, preferred_element_type=f32
        )
        total = piece if total is None else total + piece
    return total


def quarter_index(ref, flip):
    rows = ref.shape[0] // 4
    half = (lax.axis_index("ex") & 1) ^ flip
    return index_row(ref, ((lax.axis_index("rows") & 1) * 2 + half) * rows, rows)


def right_block(values, index, block_id, row_count):
    width = values.shape[1]
    row_bits = row_count.bit_length() - 1
    parts = []
    for first in range(0, index.shape[1], 512):
        group = index[:, first : first + 512]
        part = cot_products(values, group % width, 256)
        parts.append(part * parity_sign((group // width) & block_id, row_bits))
    return parts


def block_signs(sign_ref, block_id, width):
    rows = width // sign_ref.shape[1]
    return index_row(sign_ref, block_id * rows, rows).astype(bf16)


def matrix_chunk(matrix_ref, chunk, shape):
    rows, depth = shape
    half = (lax.axis_index("rows") & 1) ^ (chunk // 2)
    first = pl.multiple_of((half * 2 + (lax.axis_index("ex") & 1)) * depth, depth)
    return matrix_ref.at[pl.ds(chunk % 2 * rows, rows), pl.ds(first, depth)]


def sign_kernel(hidden_in, sign_in, out_ref, hidden_ref, sign_ref, sems):
    copies = [
        pltpu.make_async_copy(hidden_in, hidden_ref, sems.at[0]),
        pltpu.make_async_copy(sign_in, sign_ref, sems.at[1]),
    ]
    for copy in copies:
        copy.start()
    for copy in copies:
        copy.wait()
    out_ref[0] = hidden_ref[...] * sign_ref[...].astype(bf16)


def own_kernel(row_count, *refs):
    (cot_in, sign_in, col_in, row_in, len_in, matrix_ref), refs = refs[:6], refs[6:]
    right_ref, near_sign_ref, table_ref, member_ref, held_ref, col_ref, row_ref = refs[:7]
    cot_ref, sign_ref, len_ref, sems = refs[7:]
    pairs = (
        (cot_in, cot_ref),
        (sign_in, sign_ref),
        (col_in, col_ref),
        (row_in, row_ref),
        (len_in, len_ref),
        (matrix_chunk(matrix_ref, 0, held_ref.shape), held_ref),
    )
    copies = [pltpu.make_async_copy(*pair, sems.at[at]) for at, pair in enumerate(pairs)]
    for copy in copies:
        copy.start()
    for copy in copies[:-1]:
        copy.wait()
    rank = lax.axis_index("rows")
    width = cot_ref.shape[1]
    near_sign_ref[...] = block_signs(sign_ref, rank ^ 1, width)

    values = cot_ref[...] * block_signs(sign_ref, rank, width)
    for flip in range(2):
        first = 0
        for part in right_block(values, quarter_index(col_ref, flip), rank, row_count):
            right_ref[flip, :, first : first + part.shape[1]] = part
            first += part.shape[1]
    tables(row_ref, len_ref, table_ref, member_ref)
    copies[-1].wait()


def tables(row_ref, len_ref, table_ref, member_ref):
    width = table_ref.shape[1]
    for flip in range(2):
        table_ref[flip] = sign_columns(quarter_index(row_ref, flip) % width, width)
    examples, tokens = member_ref.shape
    ex_rank = lax.axis_index("ex")
    ex_count = lax.axis_size("ex")
    own = examples // ex_count
    shape = (examples, examples)
    row_id = lax.broadcasted_iota(jnp.int32, shape, 0)
    example = ((row_id // own) ^ (ex_rank & ~1) ^ (ex_count - 2)) * own + row_id % own
    other = lax.broadcasted_iota(jnp.int32, shape, 1)
    counts = jnp.broadcast_to(len_ref[...], shape)
    ends = jnp.sum(jnp.where(other <= example, counts, 0), axis=1, keepdims=True)
    starts = jnp.sum(jnp.where(other < example, counts, 0), axis=1, keepdims=True)
    position = ex_rank * tokens + lax.broadcasted_iota(jnp.int32, (examples, tokens), 1)
    inside = jnp.logical_and(position >= starts, position < ends)
    member_ref[...] = inside.astype(f32).astype(bf16)


def right_kernel(row_count, cot_ref, sign_ref, col_ref, own_ref, out_ref):
    values = cot_ref[...] * sign_ref[...]
    near = lax.axis_index("rows") ^ 1
    for flip in range(2):
        first = 0
        for part in right_block(values, quarter_index(col_ref, flip), near, row_count):
            columns = slice(first, first + part.shape[1])
            out_ref[flip, :, columns] = own_ref[flip, :, columns] + part
            first += part.shape[1]


def feature_kernel(flip, row_count, masks, hidden_refs, right_ref, row_ref, table_ref, member_ref, out_ref):
    rank = lax.axis_index("rows")
    row_bits = row_count.bit_length() - 1
    blocks = [ref[block] for ref in hidden_refs for block in range(ref.shape[0])]
    base = table_ref[flip]
    high = quarter_index(row_ref, flip) // base.shape[0]
    left = None
    for first in range(0, len(masks), 4):
        table = [
            base * parity_sign(high & (rank ^ mask), row_bits).astype(bf16)
            for mask in masks[first : first + 4]
        ]
        piece = jnp.dot(
            jnp.concatenate(blocks[first : first + 4], axis=1),
            jnp.concatenate(table, axis=0),
            preferred_element_type=f32,
        )
        left = piece if left is None else left + piece
    product = left * right_ref[flip]
    high_part = product.astype(bf16)
    low_part = (product - high_part.astype(f32)).astype(bf16)
    member = member_ref[...]
    total = jnp.dot(member, high_part, preferred_element_type=f32)
    total = total + jnp.dot(member, low_part, preferred_element_type=f32)
    out_ref[...] = total.astype(out_ref.dtype)


def load_kernel(chunk, matrix_ref, after_ref, out_ref, token_ref, sem):
    copy = pltpu.make_async_copy(matrix_chunk(matrix_ref, chunk, out_ref.shape), out_ref, sem)
    copy.start()
    token_ref[...] = jnp.zeros_like(token_ref)
    copy.wait()


def add_kernel(kept_ref, received_ref, *refs):
    total = kept_ref[...] + received_ref[...].astype(f32)
    send_ref, total_ref = refs[-2:]
    send_ref[...] = total[: send_ref.shape[0]].astype(bf16)
    total_ref[...] = total[total.shape[0] - total_ref.shape[0] :]


def low_kernel(scale, count, *refs):
    total = refs[0][...].astype(f32)
    for ref in refs[1:count]:
        total = total + ref[...].astype(f32)
    refs[-1][...] = (total * scale).astype(bf16)


def own_score_kernel(low_ref, lower_ref, upper_ref, matrix_ref, out_ref, held_ref, sem):
    copy = pltpu.make_async_copy(matrix_chunk(matrix_ref, 3, held_ref.shape), held_ref, sem)
    copy.start()

    @pl.when(lax.axis_index("rows") >= 0)
    def _():
        rows = held_ref.shape[0]
        low = low_ref[...]
        for at, ref in enumerate((lower_ref, upper_ref)):
            out_ref[:, at * rows : (at + 1) * rows] = lax.dot_general(
                low, ref[...], contract_last, preferred_element_type=f32
            )

    copy.wait()


def near_score_kernel(low_ref, lower_ref, upper_ref, sum_ref, send_ref, keep_ref):
    rows = lower_ref.shape[0]
    low = low_ref[...]
    own = low.shape[0] // 2
    lower = (lax.axis_index("ex") & 1) == 0
    for at, ref in enumerate((lower_ref, upper_ref)):
        columns = slice(at * rows, (at + 1) * rows)
        part = lax.dot_general(low, ref[...], contract_last, preferred_element_type=f32)
        part = part + sum_ref[:, columns]
        keep_ref[:, columns] = jnp.where(lower, part[:own], part[own:])
        send_ref[:, columns] = jnp.where(lower, part[own:], part[:own])


def local(hidden_acts, cotangent, lengths, row_signs, col_signs, feat_row, feat_col, inverse_rows):
    row_count = lax.axis_size("rows")
    ex_count = lax.axis_size("ex")
    tokens, width = hidden_acts.shape
    model_width = col_signs.shape[0]
    feature_count = feat_row.shape[0]
    example_count = lengths.shape[0]
    quarter = feature_count // 4
    own_examples = example_count // ex_count
    norm_scale = 1.0 / math.sqrt(width * row_count * model_width)
    whole = pl.BlockSpec(memory_space=pltpu.VMEM)
    params = pltpu.CompilerParams(vmem_limit_bytes=vmem_bytes)

    anywhere = pl.BlockSpec(memory_space=pltpu.HBM)
    out_rows = inverse_rows.shape[0]

    chunk = (out_rows // 2, quarter)
    table_shape = (feature_count // 128, 128)

    near_cot = swap(cotangent, "rows", 1)
    signed = pl.pallas_call(
        sign_kernel,
        out_shape=pltpu.VMEM((1, tokens, width), bf16),
        in_specs=[anywhere] * 2,
        out_specs=whole,
        scratch_shapes=[
            pltpu.VMEM((tokens, width), bf16),
            pltpu.VMEM((1, width), jnp.int32),
            pltpu.SemaphoreType.DMA((2,)),
        ],
        compiler_params=params,
    )(in_hbm(hidden_acts), in_hbm(row_signs.reshape(1, -1)))
    group = min(row_count, 4)
    masks = [0] + list(range(1, group))[::-1]
    hidden_parts = [signed] + [swap(signed, "rows", mask) for mask in masks[1:]]
    step = group
    while step < row_count:
        held = jnp.concatenate(hidden_parts, axis=0)
        hidden_parts = [held, swap(held, "rows", step)]
        masks += [mask | step for mask in masks]
        step *= 2
    parts = len(hidden_parts)

    cot_width = cotangent.shape[1]
    lanes = min(128, cot_width)
    right_shape = pltpu.VMEM((2, tokens, quarter), f32)
    right, near_signs, hidden_table, member, matrix_0, col_index, row_index = pl.pallas_call(
        functools.partial(own_kernel, row_count),
        out_shape=(
            right_shape,
            pltpu.VMEM((1, cot_width), bf16),
            pltpu.VMEM((2, width, quarter), bf16),
            pltpu.VMEM((example_count, tokens), bf16),
            pltpu.VMEM(chunk, bf16),
            pltpu.VMEM(table_shape, jnp.int32),
            pltpu.VMEM(table_shape, jnp.int32),
        ),
        in_specs=[anywhere] * 6,
        out_specs=(whole,) * 7,
        scratch_shapes=[
            pltpu.VMEM(cotangent.shape, bf16),
            pltpu.VMEM((model_width // lanes, lanes), jnp.int32),
            pltpu.VMEM((1, example_count), jnp.int32),
            pltpu.SemaphoreType.DMA((6,)),
        ],
        compiler_params=params,
    )(
        in_hbm(cotangent),
        in_hbm(col_signs.reshape(-1, lanes)),
        in_hbm(feat_col.reshape(-1, 128)),
        in_hbm(feat_row.reshape(-1, 128)),
        in_hbm(lengths.reshape(1, -1)),
        in_hbm(inverse_rows),
    )
    right = pl.pallas_call(
        functools.partial(right_kernel, row_count),
        out_shape=right_shape,
        in_specs=[whole] * 4,
        out_specs=whole,
        compiler_params=params,
    )(near_cot, near_signs, col_index, right)

    def features(flip):
        def kernel(*refs):
            feature_kernel(flip, row_count, masks, refs[:parts], *refs[parts:])

        return pl.pallas_call(
            kernel,
            out_shape=pltpu.VMEM((example_count, quarter), bf16 if flip else f32),
            in_specs=[whole] * (parts + 4),
            out_specs=whole,
            compiler_params=params,
        )(*hidden_parts, right, row_index, hidden_table, member)

    def load(chunk_id, after):
        return pl.pallas_call(
            functools.partial(load_kernel, chunk_id),
            out_shape=(pltpu.VMEM(chunk, bf16), pltpu.VMEM((8, 128), f32)),
            in_specs=[anywhere, whole],
            out_specs=(whole, whole),
            scratch_shapes=[pltpu.SemaphoreType.DMA],
            compiler_params=params,
        )(in_hbm(inverse_rows), after)

    def add_up(kept, received, send_count, token):
        count = received.shape[0]
        return pl.pallas_call(
            add_kernel,
            out_shape=(
                pltpu.VMEM((send_count, quarter), bf16),
                pltpu.VMEM((count - send_count % count, quarter), f32),
            ),
            in_specs=[whole] * (2 + (token is not None)),
            out_specs=(whole, whole),
            compiler_params=params,
        )(kept, received, *([] if token is None else [token]))

    def features_low(terms, token):
        return pl.pallas_call(
            functools.partial(low_kernel, norm_scale, len(terms)),
            out_shape=pltpu.VMEM(terms[0].shape, bf16),
            in_specs=[whole] * (len(terms) + (token is not None)),
            out_specs=whole,
            compiler_params=params,
        )(*terms, *([] if token is None else [token]))

    ex_masks = [1 << bit for bit in range(1, ex_count.bit_length() - 1)][::-1]
    row_masks = [1 << bit for bit in range(2, row_count.bit_length() - 1)]
    received = swap(features(1), "ex", 1)
    total = features(0)
    matrix_1, token = None, None
    for axis, mask in [("ex", mask) for mask in ex_masks] + [("rows", mask) for mask in row_masks]:
        count = received.shape[0]
        send, total = add_up(total, received, count // 2 if axis == "ex" else count, token)
        token = None
        if matrix_1 is None:
            matrix_1, token = load(1, send)
        received = swap(send, axis, mask)
    send, total = add_up(total, received, received.shape[0], token)
    matrix_2, token = load(2, send)
    others = [swap(send, "rows", mask) for mask in range(1, group)]
    low = features_low([total] + others[1:2], token)
    near_low = features_low(others[0::2][::-1], None)

    part, matrix_3 = pl.pallas_call(
        own_score_kernel,
        out_shape=(pltpu.VMEM((2 * own_examples, out_rows), f32), pltpu.VMEM(chunk, bf16)),
        in_specs=[whole] * 3 + [anywhere],
        out_specs=(whole, whole),
        scratch_shapes=[pltpu.SemaphoreType.DMA],
        compiler_params=params,
    )(low, matrix_0, matrix_1, in_hbm(inverse_rows))
    own_shape = pltpu.VMEM((own_examples, out_rows), f32)
    send, keep = pl.pallas_call(
        near_score_kernel,
        out_shape=(own_shape, own_shape),
        in_specs=[whole] * 4,
        out_specs=(whole, whole),
        compiler_params=params,
    )(near_low, matrix_2, matrix_3, part)
    return (keep + swap(send, "ex", 1)).astype(bf16)


def solution(mesh):
    placed = (
        P(("parts", "ex"), "rows"),
        P(("parts", "ex"), "rows"),
        P("parts"),
        P("rows"),
        P(),
        P(),
        P(),
        P("rows", None),
    )
    return jax.shard_map(
        local, mesh=mesh, in_specs=placed, out_specs=P(("parts", "ex"), "rows"), check_vma=False
    )
```

```python
import functools
import math

import jax
import jax.numpy as jnp
from jax import lax
from jax.experimental import pallas as pl
from jax.experimental.pallas import tpu as pltpu
from jax.sharding import PartitionSpec as P

f32 = jnp.float32
bf16 = jnp.bfloat16
contract_last = (((1,), (1,)), ((), ()))
vmem_bytes = 14 * 2**20


def in_hbm(values):
    return pltpu.with_memory_space_constraint(values, pltpu.HBM)


def swap(values, axis, mask):
    size = lax.axis_size(axis)
    return lax.ppermute(values, axis, [(rank, rank ^ mask) for rank in range(size)])


def bit_sign(index, bit_pos):
    return (1 - 2 * (index >> bit_pos & 1)).astype(f32)


def parity_sign(bits, bit_count):
    parity = bits & 1
    for bit_pos in range(1, bit_count):
        parity = parity ^ (bits >> bit_pos & 1)
    return (1 - 2 * parity).astype(f32)


def sign_columns(index, size):
    columns = index.shape[1]
    first = min(size, 16)
    row_id = lax.broadcasted_iota(jnp.int32, (first, columns), 0)
    first_bits = first.bit_length() - 1
    table = parity_sign(row_id & index, first_bits).astype(bf16)
    for bit_pos in range(first_bits, size.bit_length() - 1):
        table = jnp.concatenate([table, table * bit_sign(index, bit_pos).astype(bf16)], axis=0)
    return table


def index_row(ref, start, count):
    rows = [ref[pl.ds(start + step, 1), :] for step in range(count)]
    return jnp.concatenate(rows, axis=1)


def cot_products(values, index, block):
    size = values.shape[1]
    base_size = min(size, block)
    base = sign_columns(index, base_size)
    total = None
    for part in range(size // base_size):
        table = base
        if part > 0:
            sign = parity_sign((index // base_size) & part, (size // base_size).bit_length() - 1)
            table = base * sign.astype(bf16)
        piece = jnp.dot(
            values[:, part * base_size : (part + 1) * base_size], table, preferred_element_type=f32
        )
        total = piece if total is None else total + piece
    return total


def run_count(row_count):
    return 2 if row_count == 4 else 1


def quarter_index(ref, flip, runs):
    rank = lax.axis_index("rows")
    half = (lax.axis_index("ex") & 1) ^ flip
    rows = ref.shape[0] // 4 // runs
    if runs == 1:
        return index_row(ref, ((rank & 1) * 2 + half) * rows, rows)
    starts = [((rank ^ (2 * run)) * 2 + half) * rows for run in range(runs)]
    return jnp.concatenate([index_row(ref, start, rows) for start in starts], axis=1)


def right_block(values, index, block_id, row_count):
    width = values.shape[1]
    row_bits = row_count.bit_length() - 1
    parts = []
    for first in range(0, index.shape[1], 512):
        group = index[:, first : first + 512]
        part = cot_products(values, group % width, 256)
        parts.append(part * parity_sign((group // width) & block_id, row_bits))
    return parts


def block_signs(sign_ref, block_id, width):
    rows = width // sign_ref.shape[1]
    return index_row(sign_ref, block_id * rows, rows).astype(bf16)


def chunk_shape(chunk, out_rows, quarter, runs):
    if runs == 1:
        return (out_rows // 2, quarter)
    return (quarter // 2, out_rows) if chunk == 0 else (out_rows, quarter // 2)


def matrix_chunk(matrix_ref, chunk, shape, runs):
    rank = lax.axis_index("rows")
    core = lax.axis_index("ex") & 1
    rows, depth = shape
    if runs == 1:
        half = (rank & 1) ^ (chunk // 2)
        first = pl.multiple_of((half * 2 + core) * depth, depth)
        return matrix_ref.at[pl.ds(chunk % 2 * rows, rows), pl.ds(first, depth)]
    if chunk == 0:
        return matrix_ref.at[
            pl.ds(pl.multiple_of(core * rows, rows), rows),
            pl.ds(pl.multiple_of(rank * depth, depth), depth),
        ]
    block = rank ^ (0, 2, 1, 3)[chunk]
    return matrix_ref.at[:, pl.ds(pl.multiple_of((block * 2 + core) * depth, depth), depth)]


def sign_kernel(hidden_in, sign_in, out_ref, hidden_ref, sign_ref, sems):
    copies = [
        pltpu.make_async_copy(hidden_in, hidden_ref, sems.at[0]),
        pltpu.make_async_copy(sign_in, sign_ref, sems.at[1]),
    ]
    for copy in copies:
        copy.start()
    for copy in copies:
        copy.wait()
    out_ref[0] = hidden_ref[...] * sign_ref[...].astype(bf16)


def own_kernel(row_count, *refs):
    (cot_in, sign_in, col_in, row_in, len_in, matrix_ref), refs = refs[:6], refs[6:]
    right_ref, near_sign_ref, table_ref, member_ref, held_ref, col_ref, row_ref = refs[:7]
    cot_ref, sign_ref, len_ref, sems = refs[7:]
    pairs = (
        (cot_in, cot_ref),
        (sign_in, sign_ref),
        (col_in, col_ref),
        (row_in, row_ref),
        (len_in, len_ref),
        (matrix_chunk(matrix_ref, 0, held_ref.shape, run_count(row_count)), held_ref),
    )
    copies = [pltpu.make_async_copy(*pair, sems.at[at]) for at, pair in enumerate(pairs)]
    for copy in copies:
        copy.start()
    for copy in copies[:-1]:
        copy.wait()
    rank = lax.axis_index("rows")
    width = cot_ref.shape[1]
    near_sign_ref[...] = block_signs(sign_ref, rank ^ 1, width)

    values = cot_ref[...] * block_signs(sign_ref, rank, width)
    for flip in range(2):
        first = 0
        for part in right_block(values, quarter_index(col_ref, flip, run_count(row_count)), rank, row_count):
            right_ref[flip, :, first : first + part.shape[1]] = part
            first += part.shape[1]
    tables(row_count, row_ref, len_ref, table_ref, member_ref)
    copies[-1].wait()


def tables(row_count, row_ref, len_ref, table_ref, member_ref):
    width = table_ref.shape[1]
    for flip in range(2):
        table_ref[flip] = sign_columns(quarter_index(row_ref, flip, run_count(row_count)) % width, width)
    examples, tokens = member_ref.shape
    ex_rank = lax.axis_index("ex")
    ex_count = lax.axis_size("ex")
    own = examples // ex_count
    shape = (examples, examples)
    row_id = lax.broadcasted_iota(jnp.int32, shape, 0)
    example = ((row_id // own) ^ (ex_rank & ~1) ^ (ex_count - 2)) * own + row_id % own
    other = lax.broadcasted_iota(jnp.int32, shape, 1)
    counts = jnp.broadcast_to(len_ref[...], shape)
    ends = jnp.sum(jnp.where(other <= example, counts, 0), axis=1, keepdims=True)
    starts = jnp.sum(jnp.where(other < example, counts, 0), axis=1, keepdims=True)
    position = ex_rank * tokens + lax.broadcasted_iota(jnp.int32, (examples, tokens), 1)
    inside = jnp.logical_and(position >= starts, position < ends)
    member_ref[...] = inside.astype(f32).astype(bf16)


def right_kernel(row_count, cot_ref, sign_ref, col_ref, own_ref, out_ref):
    values = cot_ref[...] * sign_ref[...]
    near = lax.axis_index("rows") ^ 1
    for flip in range(2):
        first = 0
        for part in right_block(values, quarter_index(col_ref, flip, run_count(row_count)), near, row_count):
            columns = slice(first, first + part.shape[1])
            out_ref[flip, :, columns] = own_ref[flip, :, columns] + part
            first += part.shape[1]


def feature_kernel(flip, row_count, masks, hidden_refs, right_ref, row_ref, table_ref, member_ref, out_ref):
    rank = lax.axis_index("rows")
    row_bits = row_count.bit_length() - 1
    blocks = [ref[block] for ref in hidden_refs for block in range(ref.shape[0])]
    base = table_ref[flip]
    high = quarter_index(row_ref, flip, run_count(row_count)) // base.shape[0]
    left = None
    for first in range(0, len(masks), 4):
        table = [
            base * parity_sign(high & (rank ^ mask), row_bits).astype(bf16)
            for mask in masks[first : first + 4]
        ]
        piece = jnp.dot(
            jnp.concatenate(blocks[first : first + 4], axis=1),
            jnp.concatenate(table, axis=0),
            preferred_element_type=f32,
        )
        left = piece if left is None else left + piece
    product = left * right_ref[flip]
    high_part = product.astype(bf16)
    low_part = (product - high_part.astype(f32)).astype(bf16)
    member = member_ref[...]
    total = jnp.dot(member, high_part, preferred_element_type=f32)
    total = total + jnp.dot(member, low_part, preferred_element_type=f32)
    out_ref[...] = total.astype(out_ref.dtype)


def last_half(matrix_ref, half, shape, runs):
    rows, depth = shape
    return matrix_chunk(matrix_ref, 3, (2 * rows, depth), runs).at[pl.ds(half * rows, rows), :]


def load_kernel(chunk, runs, matrix_ref, after_ref, *refs):
    *out_refs, token_ref, sems = refs
    sources = [matrix_chunk(matrix_ref, chunk, out_refs[0].shape, runs)]
    if chunk == 2:
        sources.append(last_half(matrix_ref, 0, out_refs[1].shape, runs))
    copies = [
        pltpu.make_async_copy(source, ref, sems.at[at])
        for at, (source, ref) in enumerate(zip(sources, out_refs))
    ]
    for copy in copies:
        copy.start()
    token_ref[...] = jnp.zeros_like(token_ref)
    for copy in copies:
        copy.wait()


def add_kernel(kept_ref, received_ref, *refs):
    total = kept_ref[...] + received_ref[...].astype(f32)
    send_ref, total_ref = refs[-2:]
    send_ref[...] = total[: send_ref.shape[0]].astype(bf16)
    total_ref[...] = total[total.shape[0] - total_ref.shape[0] :]


def low_kernel(scale, turns, *refs):
    total = None
    for turn, ref in zip(turns, refs):
        term = ref[...].astype(f32)
        if turn:
            run = term.shape[1] // 2
            term = jnp.concatenate([term[:, run:], term[:, :run]], axis=1)
        total = term if total is None else total + term
    refs[-1][...] = (total * scale).astype(bf16)


def times_transposed(low, refs):
    parts = [
        lax.dot_general(low, ref[...], contract_last, preferred_element_type=f32) for ref in refs
    ]
    return parts[0] if len(parts) == 1 else jnp.concatenate(parts, axis=1)


def own_score_kernel(runs, low_ref, lower_ref, upper_ref, matrix_ref, out_ref, held_ref, sem):
    copy = pltpu.make_async_copy(last_half(matrix_ref, 1, held_ref.shape, runs), held_ref, sem)
    copy.start()

    @pl.when(lax.axis_index("rows") >= 0)
    def _():
        low = low_ref[...]
        if runs == 1:
            out_ref[...] = times_transposed(low, (lower_ref, upper_ref))
        else:
            run = low.shape[1] // 2
            straight = jnp.dot(low[:, :run], lower_ref[...], preferred_element_type=f32)
            out_ref[...] = straight + times_transposed(low[:, run:], (upper_ref,))

    copy.wait()


def near_score_kernel(runs, low_ref, lower_ref, *refs):
    *upper_refs, sum_ref, send_ref, keep_ref = refs
    low = low_ref[...]
    if runs == 1:
        part = times_transposed(low, (lower_ref, *upper_refs))
    else:
        run = low.shape[1] // 2
        part = times_transposed(low[:, :run], (lower_ref,)) + times_transposed(low[:, run:], upper_refs)
    part = part + sum_ref[...]
    own = part.shape[0] // 2
    lower = (lax.axis_index("ex") & 1) == 0
    keep_ref[...] = jnp.where(lower, part[:own], part[own:])
    send_ref[...] = jnp.where(lower, part[own:], part[:own])


def local(hidden_acts, cotangent, lengths, row_signs, col_signs, feat_row, feat_col, inverse_rows):
    row_count = lax.axis_size("rows")
    ex_count = lax.axis_size("ex")
    tokens, width = hidden_acts.shape
    model_width = col_signs.shape[0]
    feature_count = feat_row.shape[0]
    example_count = lengths.shape[0]
    quarter = feature_count // 4
    own_examples = example_count // ex_count
    norm_scale = 1.0 / math.sqrt(width * row_count * model_width)
    whole = pl.BlockSpec(memory_space=pltpu.VMEM)
    params = pltpu.CompilerParams(vmem_limit_bytes=vmem_bytes)

    anywhere = pl.BlockSpec(memory_space=pltpu.HBM)
    out_rows = inverse_rows.shape[0]

    runs = run_count(row_count)
    chunks = [pltpu.VMEM(chunk_shape(at, out_rows, quarter, runs), bf16) for at in range(4)]
    last_rows, last_depth = chunks[3].shape
    last_chunk = pltpu.VMEM((last_rows // 2, last_depth), bf16)
    table_shape = (feature_count // 128, 128)

    near_cot = swap(cotangent, "rows", 1)
    signed = pl.pallas_call(
        sign_kernel,
        out_shape=pltpu.VMEM((1, tokens, width), bf16),
        in_specs=[anywhere] * 2,
        out_specs=whole,
        scratch_shapes=[
            pltpu.VMEM((tokens, width), bf16),
            pltpu.VMEM((1, width), jnp.int32),
            pltpu.SemaphoreType.DMA((2,)),
        ],
        compiler_params=params,
    )(in_hbm(hidden_acts), in_hbm(row_signs.reshape(1, -1)))
    group = min(row_count, 4)
    masks = [0] + list(range(1, group))[::-1]
    hidden_parts = [signed] + [swap(signed, "rows", mask) for mask in masks[1:]]
    step = group
    while step < row_count:
        held = jnp.concatenate(hidden_parts, axis=0)
        hidden_parts = [held, swap(held, "rows", step)]
        masks += [mask | step for mask in masks]
        step *= 2
    parts = len(hidden_parts)

    cot_width = cotangent.shape[1]
    lanes = min(128, cot_width)
    right_shape = pltpu.VMEM((2, tokens, quarter), f32)
    right, near_signs, hidden_table, member, matrix_0, col_index, row_index = pl.pallas_call(
        functools.partial(own_kernel, row_count),
        out_shape=(
            right_shape,
            pltpu.VMEM((1, cot_width), bf16),
            pltpu.VMEM((2, width, quarter), bf16),
            pltpu.VMEM((example_count, tokens), bf16),
            chunks[0],
            pltpu.VMEM(table_shape, jnp.int32),
            pltpu.VMEM(table_shape, jnp.int32),
        ),
        in_specs=[anywhere] * 6,
        out_specs=(whole,) * 7,
        scratch_shapes=[
            pltpu.VMEM(cotangent.shape, bf16),
            pltpu.VMEM((model_width // lanes, lanes), jnp.int32),
            pltpu.VMEM((1, example_count), jnp.int32),
            pltpu.SemaphoreType.DMA((6,)),
        ],
        compiler_params=params,
    )(
        in_hbm(cotangent),
        in_hbm(col_signs.reshape(-1, lanes)),
        in_hbm(feat_col.reshape(-1, 128)),
        in_hbm(feat_row.reshape(-1, 128)),
        in_hbm(lengths.reshape(1, -1)),
        in_hbm(inverse_rows),
    )
    right = pl.pallas_call(
        functools.partial(right_kernel, row_count),
        out_shape=right_shape,
        in_specs=[whole] * 4,
        out_specs=whole,
        compiler_params=params,
    )(near_cot, near_signs, col_index, right)

    def features(flip):
        def kernel(*refs):
            feature_kernel(flip, row_count, masks, refs[:parts], *refs[parts:])

        return pl.pallas_call(
            kernel,
            out_shape=pltpu.VMEM((example_count, quarter), bf16 if flip else f32),
            in_specs=[whole] * (parts + 4),
            out_specs=whole,
            compiler_params=params,
        )(*hidden_parts, right, row_index, hidden_table, member)

    def load(chunk_id, after):
        loaded = [chunks[chunk_id]] + [last_chunk] * (chunk_id == 2)
        return pl.pallas_call(
            functools.partial(load_kernel, chunk_id, runs),
            out_shape=(*loaded, pltpu.VMEM((8, 128), f32)),
            in_specs=[anywhere, whole],
            out_specs=(whole,) * (len(loaded) + 1),
            scratch_shapes=[pltpu.SemaphoreType.DMA((len(loaded),))],
            compiler_params=params,
        )(in_hbm(inverse_rows), after)

    def add_up(kept, received, send_count, token):
        count = received.shape[0]
        return pl.pallas_call(
            add_kernel,
            out_shape=(
                pltpu.VMEM((send_count, quarter), bf16),
                pltpu.VMEM((count - send_count % count, quarter), f32),
            ),
            in_specs=[whole] * (2 + (token is not None)),
            out_specs=(whole, whole),
            compiler_params=params,
        )(kept, received, *([] if token is None else [token]))

    def features_low(terms, turns, token):
        return pl.pallas_call(
            functools.partial(low_kernel, norm_scale, turns[: len(terms)]),
            out_shape=pltpu.VMEM(terms[0].shape, bf16),
            in_specs=[whole] * (len(terms) + (token is not None)),
            out_specs=whole,
            compiler_params=params,
        )(*terms, *([] if token is None else [token]))

    ex_masks = [1 << bit for bit in range(1, ex_count.bit_length() - 1)][::-1]
    row_masks = [1 << bit for bit in range(2, row_count.bit_length() - 1)]
    received = swap(features(1), "ex", 1)
    total = features(0)
    matrix_1, token = None, None
    for axis, mask in [("ex", mask) for mask in ex_masks] + [("rows", mask) for mask in row_masks]:
        count = received.shape[0]
        send, total = add_up(total, received, count // 2 if axis == "ex" else count, token)
        token = None
        if matrix_1 is None:
            matrix_1, token = load(1, send)
        received = swap(send, axis, mask)
    send, total = add_up(total, received, received.shape[0], token)
    matrix_2, matrix_3, token = load(2, send)
    others = [swap(send, "rows", mask) for mask in range(1, group)]
    turned = runs > 1
    low = features_low([total] + others[1:2], [False, turned], token)
    near_low = features_low(others[0::2][::-1], [turned, False], None)

    part, matrix_4 = pl.pallas_call(
        functools.partial(own_score_kernel, runs),
        out_shape=(pltpu.VMEM((2 * own_examples, out_rows), f32), last_chunk),
        in_specs=[whole] * 3 + [anywhere],
        out_specs=(whole, whole),
        scratch_shapes=[pltpu.SemaphoreType.DMA],
        compiler_params=params,
    )(low, matrix_0, matrix_1, in_hbm(inverse_rows))
    own_shape = pltpu.VMEM((own_examples, out_rows), f32)
    send, keep = pl.pallas_call(
        functools.partial(near_score_kernel, runs),
        out_shape=(own_shape, own_shape),
        in_specs=[whole] * 5,
        out_specs=(whole, whole),
        compiler_params=params,
    )(near_low, matrix_2, matrix_3, matrix_4, part)
    return (keep + swap(send, "ex", 1)).astype(bf16)


def solution(mesh):
    placed = (
        P(("parts", "ex"), "rows"),
        P(("parts", "ex"), "rows"),
        P("parts"),
        P("rows"),
        P(),
        P(),
        P(),
        P("rows", None),
    )
    return jax.shard_map(
        local, mesh=mesh, in_specs=placed, out_specs=P(("parts", "ex"), "rows"), check_vma=False
    )
```

```python
import functools
import math

import jax
import jax.numpy as jnp
from jax import lax
from jax.experimental import pallas as pl
from jax.experimental.pallas import tpu as pltpu
from jax.sharding import PartitionSpec as P

f32 = jnp.float32
bf16 = jnp.bfloat16
contract_last = (((1,), (1,)), ((), ()))
vmem_bytes = 14 * 2**20


def in_hbm(values):
    return pltpu.with_memory_space_constraint(values, pltpu.HBM)


def swap(values, axis, mask):
    size = lax.axis_size(axis)
    return lax.ppermute(values, axis, [(rank, rank ^ mask) for rank in range(size)])


def bit_sign(index, bit_pos):
    return (1 - 2 * (index >> bit_pos & 1)).astype(f32)


def parity_sign(bits, bit_count):
    parity = bits & 1
    for bit_pos in range(1, bit_count):
        parity = parity ^ (bits >> bit_pos & 1)
    return (1 - 2 * parity).astype(f32)


def sign_columns(index, size):
    columns = index.shape[1]
    first = min(size, 16)
    row_id = lax.broadcasted_iota(jnp.int32, (first, columns), 0)
    first_bits = first.bit_length() - 1
    table = parity_sign(row_id & index, first_bits).astype(bf16)
    for bit_pos in range(first_bits, size.bit_length() - 1):
        table = jnp.concatenate([table, table * bit_sign(index, bit_pos).astype(bf16)], axis=0)
    return table


def index_row(ref, start, count):
    rows = [ref[pl.ds(start + step, 1), :] for step in range(count)]
    return jnp.concatenate(rows, axis=1)


def cot_products(values, index, block):
    size = values.shape[1]
    base_size = min(size, block)
    base = sign_columns(index, base_size)
    total = None
    for part in range(size // base_size):
        table = base
        if part > 0:
            sign = parity_sign((index // base_size) & part, (size // base_size).bit_length() - 1)
            table = base * sign.astype(bf16)
        piece = jnp.dot(
            values[:, part * base_size : (part + 1) * base_size], table, preferred_element_type=f32
        )
        total = piece if total is None else total + piece
    return total


def run_count(row_count):
    return 2 if row_count == 4 else 1


def quarter_index(ref, flip, runs):
    rank = lax.axis_index("rows")
    half = (lax.axis_index("ex") & 1) ^ flip
    rows = ref.shape[0] // 4 // runs
    if runs == 1:
        return index_row(ref, ((rank & 1) * 2 + half) * rows, rows)
    starts = [((rank ^ (2 * run)) * 2 + half) * rows for run in range(runs)]
    return jnp.concatenate([index_row(ref, start, rows) for start in starts], axis=1)


def right_block(values, index, block_id, row_count):
    width = values.shape[1]
    row_bits = row_count.bit_length() - 1
    parts = []
    for first in range(0, index.shape[1], 512):
        group = index[:, first : first + 512]
        part = cot_products(values, group % width, 256)
        parts.append(part * parity_sign((group // width) & block_id, row_bits))
    return parts


def block_signs(sign_ref, block_id, width):
    rows = width // sign_ref.shape[1]
    return index_row(sign_ref, block_id * rows, rows).astype(bf16)


def chunk_shape(chunk, out_rows, quarter, runs):
    if runs == 1:
        return (out_rows // 2, quarter)
    return (quarter // 2, out_rows) if chunk == 0 else (out_rows, quarter // 2)


def matrix_chunk(matrix_ref, chunk, shape, runs):
    rank = lax.axis_index("rows")
    core = lax.axis_index("ex") & 1
    rows, depth = shape
    if runs == 1:
        half = (rank & 1) ^ (chunk // 2)
        first = pl.multiple_of((half * 2 + core) * depth, depth)
        return matrix_ref.at[pl.ds(chunk % 2 * rows, rows), pl.ds(first, depth)]
    if chunk == 0:
        return matrix_ref.at[
            pl.ds(pl.multiple_of(core * rows, rows), rows),
            pl.ds(pl.multiple_of(rank * depth, depth), depth),
        ]
    block = rank ^ (0, 2, 1, 3)[chunk]
    return matrix_ref.at[:, pl.ds(pl.multiple_of((block * 2 + core) * depth, depth), depth)]


def sign_kernel(hidden_in, sign_in, out_ref, hidden_ref, sign_ref, sems):
    copies = [
        pltpu.make_async_copy(hidden_in, hidden_ref, sems.at[0]),
        pltpu.make_async_copy(sign_in, sign_ref, sems.at[1]),
    ]
    for copy in copies:
        copy.start()
    for copy in copies:
        copy.wait()
    out_ref[0] = hidden_ref[...] * sign_ref[...].astype(bf16)


def own_kernel(row_count, *refs):
    (cot_in, sign_in, col_in, row_in, len_in, matrix_ref), refs = refs[:6], refs[6:]
    right_ref, near_sign_ref, table_ref, member_ref, held_ref, last_ref, col_ref, row_ref = refs[:8]
    cot_ref, sign_ref, len_ref, sems = refs[8:]
    runs = run_count(row_count)
    pairs = (
        (cot_in, cot_ref),
        (sign_in, sign_ref),
        (col_in, col_ref),
        (row_in, row_ref),
        (len_in, len_ref),
        (matrix_chunk(matrix_ref, 2, held_ref.shape, runs), held_ref),
        (last_half(matrix_ref, 1, last_ref.shape, runs), last_ref),
    )
    copies = [pltpu.make_async_copy(*pair, sems.at[at]) for at, pair in enumerate(pairs)]
    for copy in copies:
        copy.start()
    for copy in copies[:-2]:
        copy.wait()
    rank = lax.axis_index("rows")
    width = cot_ref.shape[1]
    near_sign_ref[...] = block_signs(sign_ref, rank ^ 1, width)

    values = cot_ref[...] * block_signs(sign_ref, rank, width)
    for flip in range(2):
        first = 0
        for part in right_block(values, quarter_index(col_ref, flip, run_count(row_count)), rank, row_count):
            right_ref[flip, :, first : first + part.shape[1]] = part
            first += part.shape[1]
    tables(row_count, row_ref, len_ref, table_ref, member_ref)
    for copy in copies[-2:]:
        copy.wait()


def tables(row_count, row_ref, len_ref, table_ref, member_ref):
    width = table_ref.shape[1]
    for flip in range(2):
        table_ref[flip] = sign_columns(quarter_index(row_ref, flip, run_count(row_count)) % width, width)
    examples, tokens = member_ref.shape
    ex_rank = lax.axis_index("ex")
    ex_count = lax.axis_size("ex")
    own = examples // ex_count
    shape = (examples, examples)
    row_id = lax.broadcasted_iota(jnp.int32, shape, 0)
    example = ((row_id // own) ^ (ex_rank & ~1) ^ (ex_count - 2)) * own + row_id % own
    other = lax.broadcasted_iota(jnp.int32, shape, 1)
    counts = jnp.broadcast_to(len_ref[...], shape)
    ends = jnp.sum(jnp.where(other <= example, counts, 0), axis=1, keepdims=True)
    starts = jnp.sum(jnp.where(other < example, counts, 0), axis=1, keepdims=True)
    position = ex_rank * tokens + lax.broadcasted_iota(jnp.int32, (examples, tokens), 1)
    inside = jnp.logical_and(position >= starts, position < ends)
    member_ref[...] = inside.astype(f32).astype(bf16)


def right_kernel(row_count, cot_ref, sign_ref, col_ref, own_ref, matrix_ref, out_ref, last_ref, sem):
    runs = run_count(row_count)
    copy = pltpu.make_async_copy(last_half(matrix_ref, 0, last_ref.shape, runs), last_ref, sem)
    copy.start()
    rank = lax.axis_index("rows")

    @pl.when(rank >= 0)
    def _():
        values = cot_ref[...] * sign_ref[...]
        for flip in range(2):
            first = 0
            for part in right_block(values, quarter_index(col_ref, flip, runs), rank ^ 1, row_count):
                columns = slice(first, first + part.shape[1])
                out_ref[flip, :, columns] = own_ref[flip, :, columns] + part
                first += part.shape[1]

    copy.wait()


def feature_kernel(flip, row_count, masks, hidden_refs, right_ref, row_ref, table_ref, member_ref, out_ref):
    rank = lax.axis_index("rows")
    row_bits = row_count.bit_length() - 1
    blocks = [ref[block] for ref in hidden_refs for block in range(ref.shape[0])]
    base = table_ref[flip]
    high = quarter_index(row_ref, flip, run_count(row_count)) // base.shape[0]
    left = None
    for first in range(0, len(masks), 4):
        table = [
            base * parity_sign(high & (rank ^ mask), row_bits).astype(bf16)
            for mask in masks[first : first + 4]
        ]
        piece = jnp.dot(
            jnp.concatenate(blocks[first : first + 4], axis=1),
            jnp.concatenate(table, axis=0),
            preferred_element_type=f32,
        )
        left = piece if left is None else left + piece
    product = left * right_ref[flip]
    high_part = product.astype(bf16)
    low_part = (product - high_part.astype(f32)).astype(bf16)
    member = member_ref[...]
    total = jnp.dot(member, high_part, preferred_element_type=f32)
    total = total + jnp.dot(member, low_part, preferred_element_type=f32)
    out_ref[...] = total.astype(out_ref.dtype)


def last_half(matrix_ref, half, shape, runs):
    rows, depth = shape
    return matrix_chunk(matrix_ref, 3, (2 * rows, depth), runs).at[pl.ds(half * rows, rows), :]


def turn_kernel(chunk, runs, given, matrix_ref, after_ref, *refs):
    given_refs, (out_ref, *turned_refs, token_ref, sem) = refs[:given], refs[given:]
    copy = pltpu.make_async_copy(matrix_chunk(matrix_ref, chunk, out_ref.shape, runs), out_ref, sem)
    copy.start()
    token_ref[...] = jnp.zeros_like(token_ref)

    @pl.when(lax.axis_index("rows") >= 0)
    def _():
        for given_ref, turned_ref in zip(given_refs, turned_refs):
            depth = turned_ref.shape[0]
            block = math.gcd(depth, 256)
            shape = (block, block)
            same = lax.broadcasted_iota(jnp.int32, shape, 0) == lax.broadcasted_iota(jnp.int32, shape, 1)
            identity = same.astype(f32).astype(bf16)
            for first in range(0, depth, block):
                turned_ref[first : first + block, :] = lax.dot_general(
                    identity,
                    given_ref[:, first : first + block],
                    contract_last,
                    preferred_element_type=f32,
                ).astype(bf16)

    copy.wait()


def add_kernel(kept_ref, received_ref, *refs):
    total = kept_ref[...] + received_ref[...].astype(f32)
    send_ref, total_ref = refs[-2:]
    send_ref[...] = total[: send_ref.shape[0]].astype(bf16)
    total_ref[...] = total[total.shape[0] - total_ref.shape[0] :]


def low_kernel(scale, turns, *refs):
    total = None
    for turn, ref in zip(turns, refs):
        term = ref[...].astype(f32)
        if turn:
            run = term.shape[1] // 2
            term = jnp.concatenate([term[:, run:], term[:, :run]], axis=1)
        total = term if total is None else total + term
    refs[-1][...] = (total * scale).astype(bf16)


def times_transposed(low, refs):
    parts = [
        lax.dot_general(low, ref[...], contract_last, preferred_element_type=f32) for ref in refs
    ]
    return parts[0] if len(parts) == 1 else jnp.concatenate(parts, axis=1)


def own_score_kernel(runs, low_ref, lower_ref, upper_ref, out_ref):
    low = low_ref[...]
    if runs == 1:
        out_ref[...] = times_transposed(low, (lower_ref, upper_ref))
    else:
        run = low.shape[1] // 2
        part = jnp.dot(low[:, :run], lower_ref[...], preferred_element_type=f32)
        out_ref[...] = part + jnp.dot(low[:, run:], upper_ref[...], preferred_element_type=f32)


def near_score_kernel(runs, low_ref, lower_ref, upper_ref, last_ref, sum_ref, send_ref, keep_ref):
    low = low_ref[...]
    if runs == 1:
        part = times_transposed(low, (lower_ref, upper_ref, last_ref))
    else:
        run = low.shape[1] // 2
        part = jnp.dot(low[:, :run], lower_ref[...], preferred_element_type=f32)
        halves = [
            jnp.dot(low[:, run:], ref[...], preferred_element_type=f32) for ref in (upper_ref, last_ref)
        ]
        part = part + jnp.concatenate(halves, axis=1)
    part = part + sum_ref[...]
    own = part.shape[0] // 2
    lower = (lax.axis_index("ex") & 1) == 0
    keep_ref[...] = jnp.where(lower, part[:own], part[own:])
    send_ref[...] = jnp.where(lower, part[own:], part[:own])


def local(hidden_acts, cotangent, lengths, row_signs, col_signs, feat_row, feat_col, inverse_rows):
    row_count = lax.axis_size("rows")
    ex_count = lax.axis_size("ex")
    tokens, width = hidden_acts.shape
    model_width = col_signs.shape[0]
    feature_count = feat_row.shape[0]
    example_count = lengths.shape[0]
    quarter = feature_count // 4
    own_examples = example_count // ex_count
    norm_scale = 1.0 / math.sqrt(width * row_count * model_width)
    whole = pl.BlockSpec(memory_space=pltpu.VMEM)
    params = pltpu.CompilerParams(vmem_limit_bytes=vmem_bytes)

    anywhere = pl.BlockSpec(memory_space=pltpu.HBM)
    out_rows = inverse_rows.shape[0]

    runs = run_count(row_count)
    chunks = [pltpu.VMEM(chunk_shape(at, out_rows, quarter, runs), bf16) for at in range(4)]
    last_rows, last_depth = chunks[3].shape
    last_chunk = pltpu.VMEM((last_rows // 2, last_depth), bf16)
    table_shape = (feature_count // 128, 128)

    near_cot = swap(cotangent, "rows", 1)
    signed = pl.pallas_call(
        sign_kernel,
        out_shape=pltpu.VMEM((1, tokens, width), bf16),
        in_specs=[anywhere] * 2,
        out_specs=whole,
        scratch_shapes=[
            pltpu.VMEM((tokens, width), bf16),
            pltpu.VMEM((1, width), jnp.int32),
            pltpu.SemaphoreType.DMA((2,)),
        ],
        compiler_params=params,
    )(in_hbm(hidden_acts), in_hbm(row_signs.reshape(1, -1)))
    group = min(row_count, 4)
    masks = [0] + list(range(1, group))[::-1]
    hidden_parts = [signed] + [swap(signed, "rows", mask) for mask in masks[1:]]
    step = group
    while step < row_count:
        held = jnp.concatenate(hidden_parts, axis=0)
        hidden_parts = [held, swap(held, "rows", step)]
        masks += [mask | step for mask in masks]
        step *= 2
    parts = len(hidden_parts)

    cot_width = cotangent.shape[1]
    lanes = min(128, cot_width)
    right_shape = pltpu.VMEM((2, tokens, quarter), f32)
    right, near_signs, hidden_table, member, matrix_2, matrix_4, col_index, row_index = pl.pallas_call(
        functools.partial(own_kernel, row_count),
        out_shape=(
            right_shape,
            pltpu.VMEM((1, cot_width), bf16),
            pltpu.VMEM((2, width, quarter), bf16),
            pltpu.VMEM((example_count, tokens), bf16),
            chunks[2],
            last_chunk,
            pltpu.VMEM(table_shape, jnp.int32),
            pltpu.VMEM(table_shape, jnp.int32),
        ),
        in_specs=[anywhere] * 6,
        out_specs=(whole,) * 8,
        scratch_shapes=[
            pltpu.VMEM(cotangent.shape, bf16),
            pltpu.VMEM((model_width // lanes, lanes), jnp.int32),
            pltpu.VMEM((1, example_count), jnp.int32),
            pltpu.SemaphoreType.DMA((7,)),
        ],
        compiler_params=params,
    )(
        in_hbm(cotangent),
        in_hbm(col_signs.reshape(-1, lanes)),
        in_hbm(feat_col.reshape(-1, 128)),
        in_hbm(feat_row.reshape(-1, 128)),
        in_hbm(lengths.reshape(1, -1)),
        in_hbm(inverse_rows),
    )
    right, matrix_3 = pl.pallas_call(
        functools.partial(right_kernel, row_count),
        out_shape=(right_shape, last_chunk),
        in_specs=[whole] * 4 + [anywhere],
        out_specs=(whole, whole),
        scratch_shapes=[pltpu.SemaphoreType.DMA],
        compiler_params=params,
    )(near_cot, near_signs, col_index, right, in_hbm(inverse_rows))

    def features(flip):
        def kernel(*refs):
            feature_kernel(flip, row_count, masks, refs[:parts], *refs[parts:])

        return pl.pallas_call(
            kernel,
            out_shape=pltpu.VMEM((example_count, quarter), bf16 if flip else f32),
            in_specs=[whole] * (parts + 4),
            out_specs=whole,
            compiler_params=params,
        )(*hidden_parts, right, row_index, hidden_table, member)

    token_shape = pltpu.VMEM((8, 128), f32)

    def load_and_turn(chunk, after, given):
        turned = [pltpu.VMEM(values.shape[::-1], bf16) for values in given] if runs > 1 else []
        loaded, *outs, token = pl.pallas_call(
            functools.partial(turn_kernel, chunk, runs, len(given)),
            out_shape=(chunks[chunk], *turned, token_shape),
            in_specs=[anywhere] + [whole] * (1 + len(given)),
            out_specs=(whole,) * (len(turned) + 2),
            scratch_shapes=[pltpu.SemaphoreType.DMA],
            compiler_params=params,
        )(in_hbm(inverse_rows), after, *given)
        return loaded, outs if turned else given, token

    def add_up(kept, received, send_count, token):
        count = received.shape[0]
        return pl.pallas_call(
            add_kernel,
            out_shape=(
                pltpu.VMEM((send_count, quarter), bf16),
                pltpu.VMEM((count - send_count % count, quarter), f32),
            ),
            in_specs=[whole] * (2 + (token is not None)),
            out_specs=(whole, whole),
            compiler_params=params,
        )(kept, received, *([] if token is None else [token]))

    def features_low(terms, turns, token):
        return pl.pallas_call(
            functools.partial(low_kernel, norm_scale, turns[: len(terms)]),
            out_shape=pltpu.VMEM(terms[0].shape, bf16),
            in_specs=[whole] * (len(terms) + (token is not None)),
            out_specs=whole,
            compiler_params=params,
        )(*terms, *([] if token is None else [token]))

    ex_masks = [1 << bit for bit in range(1, ex_count.bit_length() - 1)][::-1]
    row_masks = [1 << bit for bit in range(2, row_count.bit_length() - 1)]
    received = swap(features(1), "ex", 1)
    total = features(0)
    matrix_1, token = None, None
    for axis, mask in [("ex", mask) for mask in ex_masks] + [("rows", mask) for mask in row_masks]:
        count = received.shape[0]
        send, total = add_up(total, received, count // 2 if axis == "ex" else count, token)
        token = None
        if matrix_1 is None:
            matrix_1, (matrix_2, matrix_4), token = load_and_turn(1, send, [matrix_2, matrix_4])
        received = swap(send, axis, mask)
    send, total = add_up(total, received, received.shape[0], token)
    matrix_0, (matrix_1, matrix_3), token = load_and_turn(0, send, [matrix_1, matrix_3])
    others = [swap(send, "rows", mask) for mask in range(1, group)]
    turned = runs > 1
    low = features_low([total] + others[1:2], [False, turned], token)
    near_low = features_low(others[0::2][::-1], [turned, False], None)

    part = pl.pallas_call(
        functools.partial(own_score_kernel, runs),
        out_shape=pltpu.VMEM((2 * own_examples, out_rows), f32),
        in_specs=[whole] * 3,
        out_specs=whole,
        compiler_params=params,
    )(low, matrix_0, matrix_1)
    own_shape = pltpu.VMEM((own_examples, out_rows), f32)
    send, keep = pl.pallas_call(
        functools.partial(near_score_kernel, runs),
        out_shape=(own_shape, own_shape),
        in_specs=[whole] * 5,
        out_specs=(whole, whole),
        compiler_params=params,
    )(near_low, matrix_2, matrix_3, matrix_4, part)
    return (keep + swap(send, "ex", 1)).astype(bf16)


def solution(mesh):
    placed = (
        P(("parts", "ex"), "rows"),
        P(("parts", "ex"), "rows"),
        P("parts"),
        P("rows"),
        P(),
        P(),
        P(),
        P("rows", None),
    )
    return jax.shard_map(
        local, mesh=mesh, in_specs=placed, out_specs=P(("parts", "ex"), "rows"), check_vma=False
    )
```

```python
import functools
import math

import jax
import jax.numpy as jnp
from jax import lax
from jax.experimental import pallas as pl
from jax.experimental.pallas import tpu as pltpu
from jax.sharding import PartitionSpec as P

f32 = jnp.float32
bf16 = jnp.bfloat16
contract_last = (((1,), (1,)), ((), ()))
vmem_bytes = 14 * 2**20


def in_hbm(values):
    return pltpu.with_memory_space_constraint(values, pltpu.HBM)


def swap(values, axis, mask):
    size = lax.axis_size(axis)
    return lax.ppermute(values, axis, [(rank, rank ^ mask) for rank in range(size)])


def bit_sign(index, bit_pos):
    return (1 - 2 * (index >> bit_pos & 1)).astype(f32)


def parity_sign(bits, bit_count):
    parity = bits & 1
    for bit_pos in range(1, bit_count):
        parity = parity ^ (bits >> bit_pos & 1)
    return (1 - 2 * parity).astype(f32)


def sign_columns(index, size):
    columns = index.shape[1]
    first = min(size, 16)
    row_id = lax.broadcasted_iota(jnp.int32, (first, columns), 0)
    first_bits = first.bit_length() - 1
    table = parity_sign(row_id & index, first_bits).astype(bf16)
    for bit_pos in range(first_bits, size.bit_length() - 1):
        table = jnp.concatenate([table, table * bit_sign(index, bit_pos).astype(bf16)], axis=0)
    return table


def index_row(ref, start, count):
    rows = [ref[pl.ds(start + step, 1), :] for step in range(count)]
    return jnp.concatenate(rows, axis=1)


def cot_products(values, index, block):
    size = values.shape[1]
    base_size = min(size, block)
    base = sign_columns(index, base_size)
    total = None
    for part in range(size // base_size):
        table = base
        if part > 0:
            sign = parity_sign((index // base_size) & part, (size // base_size).bit_length() - 1)
            table = base * sign.astype(bf16)
        piece = jnp.dot(
            values[:, part * base_size : (part + 1) * base_size], table, preferred_element_type=f32
        )
        total = piece if total is None else total + piece
    return total


def run_count(row_count):
    return 2 if row_count == 4 else 1


def quarter_index(ref, flip, runs):
    rank = lax.axis_index("rows")
    half = (lax.axis_index("ex") & 1) ^ flip
    rows = ref.shape[0] // 4 // runs
    if runs == 1:
        return index_row(ref, ((rank & 1) * 2 + half) * rows, rows)
    starts = [((rank ^ (2 * run)) * 2 + half) * rows for run in range(runs)]
    return jnp.concatenate([index_row(ref, start, rows) for start in starts], axis=1)


def right_block(values, index, block_id, row_count):
    width = values.shape[1]
    row_bits = row_count.bit_length() - 1
    parts = []
    for first in range(0, index.shape[1], 512):
        group = index[:, first : first + 512]
        part = cot_products(values, group % width, 256)
        parts.append(part * parity_sign((group // width) & block_id, row_bits))
    return parts


def block_signs(sign_ref, block_id, width):
    rows = width // sign_ref.shape[1]
    return index_row(sign_ref, block_id * rows, rows).astype(bf16)


def chunk_shape(chunk, out_rows, quarter, runs):
    if runs == 1:
        return (out_rows // 2, quarter)
    return (quarter // 2, out_rows) if chunk == 0 else (out_rows, quarter // 2)


def matrix_chunk(matrix_ref, chunk, shape, runs):
    rank = lax.axis_index("rows")
    core = lax.axis_index("ex") & 1
    rows, depth = shape
    if runs == 1:
        half = (rank & 1) ^ (chunk // 2)
        first = pl.multiple_of((half * 2 + core) * depth, depth)
        return matrix_ref.at[pl.ds(chunk % 2 * rows, rows), pl.ds(first, depth)]
    if chunk == 0:
        return matrix_ref.at[
            pl.ds(pl.multiple_of(core * rows, rows), rows),
            pl.ds(pl.multiple_of(rank * depth, depth), depth),
        ]
    block = rank ^ (0, 2, 1, 3)[chunk]
    return matrix_ref.at[:, pl.ds(pl.multiple_of((block * 2 + core) * depth, depth), depth)]


def sign_kernel(hidden_in, sign_in, out_ref, hidden_ref, sign_ref, sems):
    copies = [
        pltpu.make_async_copy(hidden_in, hidden_ref, sems.at[0]),
        pltpu.make_async_copy(sign_in, sign_ref, sems.at[1]),
    ]
    for copy in copies:
        copy.start()
    for copy in copies:
        copy.wait()
    out_ref[0] = hidden_ref[...] * sign_ref[...].astype(bf16)


def own_kernel(row_count, *refs):
    (cot_in, sign_in, col_in, row_in, len_in, matrix_ref), refs = refs[:6], refs[6:]
    right_ref, near_sign_ref, table_ref, member_ref, held_ref, last_ref, col_ref, row_ref = refs[:8]
    cot_ref, sign_ref, len_ref, sems = refs[8:]
    runs = run_count(row_count)
    pairs = (
        (cot_in, cot_ref),
        (sign_in, sign_ref),
        (col_in, col_ref),
        (row_in, row_ref),
        (len_in, len_ref),
        (matrix_chunk(matrix_ref, 2, held_ref.shape, runs), held_ref),
        (matrix_chunk(matrix_ref, 3, last_ref.shape, runs), last_ref),
    )
    copies = [pltpu.make_async_copy(*pair, sems.at[at]) for at, pair in enumerate(pairs)]
    for copy in copies:
        copy.start()
    for copy in copies[:-2]:
        copy.wait()
    rank = lax.axis_index("rows")
    width = cot_ref.shape[1]
    near_sign_ref[...] = block_signs(sign_ref, rank ^ 1, width)

    values = cot_ref[...] * block_signs(sign_ref, rank, width)
    for flip in range(2):
        first = 0
        for part in right_block(values, quarter_index(col_ref, flip, run_count(row_count)), rank, row_count):
            right_ref[flip, :, first : first + part.shape[1]] = part
            first += part.shape[1]
    tables(row_count, row_ref, len_ref, table_ref, member_ref)
    for copy in copies[-2:]:
        copy.wait()


def tables(row_count, row_ref, len_ref, table_ref, member_ref):
    width = table_ref.shape[1]
    for flip in range(2):
        table_ref[flip] = sign_columns(quarter_index(row_ref, flip, run_count(row_count)) % width, width)
    examples, tokens = member_ref.shape
    ex_rank = lax.axis_index("ex")
    ex_count = lax.axis_size("ex")
    own = examples // ex_count
    shape = (examples, examples)
    row_id = lax.broadcasted_iota(jnp.int32, shape, 0)
    example = ((row_id // own) ^ (ex_rank & ~1) ^ (ex_count - 2)) * own + row_id % own
    other = lax.broadcasted_iota(jnp.int32, shape, 1)
    counts = jnp.broadcast_to(len_ref[...], shape)
    ends = jnp.sum(jnp.where(other <= example, counts, 0), axis=1, keepdims=True)
    starts = jnp.sum(jnp.where(other < example, counts, 0), axis=1, keepdims=True)
    position = ex_rank * tokens + lax.broadcasted_iota(jnp.int32, (examples, tokens), 1)
    inside = jnp.logical_and(position >= starts, position < ends)
    member_ref[...] = inside.astype(f32).astype(bf16)


def right_kernel(row_count, cot_ref, sign_ref, col_ref, own_ref, out_ref):
    values = cot_ref[...] * sign_ref[...]
    near = lax.axis_index("rows") ^ 1
    for flip in range(2):
        first = 0
        for part in right_block(values, quarter_index(col_ref, flip, run_count(row_count)), near, row_count):
            columns = slice(first, first + part.shape[1])
            out_ref[flip, :, columns] = own_ref[flip, :, columns] + part
            first += part.shape[1]


def feature_kernel(flip, row_count, masks, hidden_refs, right_ref, row_ref, table_ref, member_ref, out_ref):
    rank = lax.axis_index("rows")
    row_bits = row_count.bit_length() - 1
    blocks = [ref[block] for ref in hidden_refs for block in range(ref.shape[0])]
    base = table_ref[flip]
    high = quarter_index(row_ref, flip, run_count(row_count)) // base.shape[0]
    left = None
    for first in range(0, len(masks), 4):
        table = [
            base * parity_sign(high & (rank ^ mask), row_bits).astype(bf16)
            for mask in masks[first : first + 4]
        ]
        piece = jnp.dot(
            jnp.concatenate(blocks[first : first + 4], axis=1),
            jnp.concatenate(table, axis=0),
            preferred_element_type=f32,
        )
        left = piece if left is None else left + piece
    product = left * right_ref[flip]
    high_part = product.astype(bf16)
    low_part = (product - high_part.astype(f32)).astype(bf16)
    member = member_ref[...]
    total = jnp.dot(member, high_part, preferred_element_type=f32)
    total = total + jnp.dot(member, low_part, preferred_element_type=f32)
    out_ref[...] = total.astype(out_ref.dtype)


def turn_kernel(chunk, runs, given, matrix_ref, after_ref, *refs):
    given_refs, (out_ref, *turned_refs, token_ref, sem) = refs[:given], refs[given:]
    copy = pltpu.make_async_copy(matrix_chunk(matrix_ref, chunk, out_ref.shape, runs), out_ref, sem)
    copy.start()
    token_ref[...] = jnp.zeros_like(token_ref)

    @pl.when(lax.axis_index("rows") >= 0)
    def _():
        for given_ref, turned_ref in zip(given_refs, turned_refs):
            depth = turned_ref.shape[0]
            block = math.gcd(depth, 256)
            shape = (block, block)
            same = lax.broadcasted_iota(jnp.int32, shape, 0) == lax.broadcasted_iota(jnp.int32, shape, 1)
            identity = same.astype(f32).astype(bf16)
            for first in range(0, depth, block):
                turned_ref[first : first + block, :] = lax.dot_general(
                    identity,
                    given_ref[:, first : first + block],
                    contract_last,
                    preferred_element_type=f32,
                ).astype(bf16)

    copy.wait()


def add_kernel(kept_ref, received_ref, *refs):
    total = kept_ref[...] + received_ref[...].astype(f32)
    send_ref, total_ref = refs[-2:]
    send_ref[...] = total[: send_ref.shape[0]].astype(bf16)
    total_ref[...] = total[total.shape[0] - total_ref.shape[0] :]


def low_kernel(scale, turns, *refs):
    total = None
    for turn, ref in zip(turns, refs):
        term = ref[...].astype(f32)
        if turn:
            run = term.shape[1] // 2
            term = jnp.concatenate([term[:, run:], term[:, :run]], axis=1)
        total = term if total is None else total + term
    refs[-1][...] = (total * scale).astype(bf16)


def products(low, lower_ref, upper_ref, runs):
    if runs == 1:
        parts = [
            lax.dot_general(low, ref[...], contract_last, preferred_element_type=f32)
            for ref in (lower_ref, upper_ref)
        ]
        return jnp.concatenate(parts, axis=1)
    run = low.shape[1] // 2
    part = jnp.dot(low[:, :run], lower_ref[...], preferred_element_type=f32)
    return part + jnp.dot(low[:, run:], upper_ref[...], preferred_element_type=f32)


def own_score_kernel(runs, low_ref, lower_ref, upper_ref, out_ref):
    out_ref[...] = products(low_ref[...], lower_ref, upper_ref, runs)


def near_score_kernel(runs, low_ref, lower_ref, upper_ref, sum_ref, send_ref, keep_ref):
    part = sum_ref[...] + products(low_ref[...], lower_ref, upper_ref, runs)
    own = part.shape[0] // 2
    lower = (lax.axis_index("ex") & 1) == 0
    keep_ref[...] = jnp.where(lower, part[:own], part[own:])
    send_ref[...] = jnp.where(lower, part[own:], part[:own])


def local(hidden_acts, cotangent, lengths, row_signs, col_signs, feat_row, feat_col, inverse_rows):
    row_count = lax.axis_size("rows")
    ex_count = lax.axis_size("ex")
    tokens, width = hidden_acts.shape
    model_width = col_signs.shape[0]
    feature_count = feat_row.shape[0]
    example_count = lengths.shape[0]
    quarter = feature_count // 4
    own_examples = example_count // ex_count
    norm_scale = 1.0 / math.sqrt(width * row_count * model_width)
    whole = pl.BlockSpec(memory_space=pltpu.VMEM)
    params = pltpu.CompilerParams(vmem_limit_bytes=vmem_bytes)

    anywhere = pl.BlockSpec(memory_space=pltpu.HBM)
    out_rows = inverse_rows.shape[0]

    runs = run_count(row_count)
    chunks = [pltpu.VMEM(chunk_shape(at, out_rows, quarter, runs), bf16) for at in range(4)]
    table_shape = (feature_count // 128, 128)

    near_cot = swap(cotangent, "rows", 1)
    signed = pl.pallas_call(
        sign_kernel,
        out_shape=pltpu.VMEM((1, tokens, width), bf16),
        in_specs=[anywhere] * 2,
        out_specs=whole,
        scratch_shapes=[
            pltpu.VMEM((tokens, width), bf16),
            pltpu.VMEM((1, width), jnp.int32),
            pltpu.SemaphoreType.DMA((2,)),
        ],
        compiler_params=params,
    )(in_hbm(hidden_acts), in_hbm(row_signs.reshape(1, -1)))
    group = min(row_count, 4)
    masks = [0] + list(range(1, group))[::-1]
    hidden_parts = [signed] + [swap(signed, "rows", mask) for mask in masks[1:]]
    step = group
    while step < row_count:
        held = jnp.concatenate(hidden_parts, axis=0)
        hidden_parts = [held, swap(held, "rows", step)]
        masks += [mask | step for mask in masks]
        step *= 2
    parts = len(hidden_parts)

    cot_width = cotangent.shape[1]
    lanes = min(128, cot_width)
    right_shape = pltpu.VMEM((2, tokens, quarter), f32)
    right, near_signs, hidden_table, member, matrix_2, matrix_3, col_index, row_index = pl.pallas_call(
        functools.partial(own_kernel, row_count),
        out_shape=(
            right_shape,
            pltpu.VMEM((1, cot_width), bf16),
            pltpu.VMEM((2, width, quarter), bf16),
            pltpu.VMEM((example_count, tokens), bf16),
            chunks[2],
            chunks[3],
            pltpu.VMEM(table_shape, jnp.int32),
            pltpu.VMEM(table_shape, jnp.int32),
        ),
        in_specs=[anywhere] * 6,
        out_specs=(whole,) * 8,
        scratch_shapes=[
            pltpu.VMEM(cotangent.shape, bf16),
            pltpu.VMEM((model_width // lanes, lanes), jnp.int32),
            pltpu.VMEM((1, example_count), jnp.int32),
            pltpu.SemaphoreType.DMA((7,)),
        ],
        compiler_params=params,
    )(
        in_hbm(cotangent),
        in_hbm(col_signs.reshape(-1, lanes)),
        in_hbm(feat_col.reshape(-1, 128)),
        in_hbm(feat_row.reshape(-1, 128)),
        in_hbm(lengths.reshape(1, -1)),
        in_hbm(inverse_rows),
    )
    right = pl.pallas_call(
        functools.partial(right_kernel, row_count),
        out_shape=right_shape,
        in_specs=[whole] * 4,
        out_specs=whole,
        compiler_params=params,
    )(near_cot, near_signs, col_index, right)

    def features(flip):
        def kernel(*refs):
            feature_kernel(flip, row_count, masks, refs[:parts], *refs[parts:])

        return pl.pallas_call(
            kernel,
            out_shape=pltpu.VMEM((example_count, quarter), bf16 if flip else f32),
            in_specs=[whole] * (parts + 4),
            out_specs=whole,
            compiler_params=params,
        )(*hidden_parts, right, row_index, hidden_table, member)

    token_shape = pltpu.VMEM((8, 128), f32)

    def load_and_turn(chunk, after, given):
        turned = [pltpu.VMEM(values.shape[::-1], bf16) for values in given] if runs > 1 else []
        loaded, *outs, token = pl.pallas_call(
            functools.partial(turn_kernel, chunk, runs, len(given)),
            out_shape=(chunks[chunk], *turned, token_shape),
            in_specs=[anywhere] + [whole] * (1 + len(given)),
            out_specs=(whole,) * (len(turned) + 2),
            scratch_shapes=[pltpu.SemaphoreType.DMA],
            compiler_params=params,
        )(in_hbm(inverse_rows), after, *given)
        return loaded, outs if turned else given, token

    def add_up(kept, received, send_count, token):
        count = received.shape[0]
        return pl.pallas_call(
            add_kernel,
            out_shape=(
                pltpu.VMEM((send_count, quarter), bf16),
                pltpu.VMEM((count - send_count % count, quarter), f32),
            ),
            in_specs=[whole] * (2 + (token is not None)),
            out_specs=(whole, whole),
            compiler_params=params,
        )(kept, received, *([] if token is None else [token]))

    def features_low(terms, turns, token):
        return pl.pallas_call(
            functools.partial(low_kernel, norm_scale, turns[: len(terms)]),
            out_shape=pltpu.VMEM(terms[0].shape, bf16),
            in_specs=[whole] * (len(terms) + (token is not None)),
            out_specs=whole,
            compiler_params=params,
        )(*terms, *([] if token is None else [token]))

    ex_masks = [1 << bit for bit in range(1, ex_count.bit_length() - 1)][::-1]
    row_masks = [1 << bit for bit in range(2, row_count.bit_length() - 1)]
    received = swap(features(1), "ex", 1)
    total = features(0)
    matrix_1, token = None, None
    for axis, mask in [("ex", mask) for mask in ex_masks] + [("rows", mask) for mask in row_masks]:
        count = received.shape[0]
        send, total = add_up(total, received, count // 2 if axis == "ex" else count, token)
        token = None
        if matrix_1 is None:
            matrix_1, (matrix_2,), token = load_and_turn(1, send, [matrix_2])
        received = swap(send, axis, mask)
    send, total = add_up(total, received, received.shape[0], token)
    matrix_0, (matrix_1, matrix_3), token = load_and_turn(0, send, [matrix_1, matrix_3])
    others = [swap(send, "rows", mask) for mask in range(1, group)]
    turned = runs > 1
    low = features_low([total] + others[1:2], [False, turned], token)
    near_low = features_low(others[0::2][::-1], [turned, False], None)

    part = pl.pallas_call(
        functools.partial(own_score_kernel, runs),
        out_shape=pltpu.VMEM((2 * own_examples, out_rows), f32),
        in_specs=[whole] * 3,
        out_specs=whole,
        compiler_params=params,
    )(low, matrix_0, matrix_1)
    own_shape = pltpu.VMEM((own_examples, out_rows), f32)
    send, keep = pl.pallas_call(
        functools.partial(near_score_kernel, runs),
        out_shape=(own_shape, own_shape),
        in_specs=[whole] * 4,
        out_specs=(whole, whole),
        compiler_params=params,
    )(near_low, matrix_2, matrix_3, part)
    return (keep + swap(send, "ex", 1)).astype(bf16)


def solution(mesh):
    placed = (
        P(("parts", "ex"), "rows"),
        P(("parts", "ex"), "rows"),
        P("parts"),
        P("rows"),
        P(),
        P(),
        P(),
        P("rows", None),
    )
    return jax.shard_map(
        local, mesh=mesh, in_specs=placed, out_specs=P(("parts", "ex"), "rows"), check_vma=False
    )
```

```python
import functools
import math

import jax
import jax.numpy as jnp
from jax import lax
from jax.experimental import pallas as pl
from jax.experimental.pallas import tpu as pltpu
from jax.sharding import PartitionSpec as P

f32 = jnp.float32
bf16 = jnp.bfloat16
contract_last = (((1,), (1,)), ((), ()))
vmem_bytes = 14 * 2**20


def in_hbm(values):
    return pltpu.with_memory_space_constraint(values, pltpu.HBM)


def swap(values, axis, mask):
    size = lax.axis_size(axis)
    return lax.ppermute(values, axis, [(rank, rank ^ mask) for rank in range(size)])


def bit_sign(index, bit_pos):
    return (1 - 2 * (index >> bit_pos & 1)).astype(f32)


def parity_sign(bits, bit_count):
    parity = bits & 1
    for bit_pos in range(1, bit_count):
        parity = parity ^ (bits >> bit_pos & 1)
    return (1 - 2 * parity).astype(f32)


def sign_columns(index, size):
    columns = index.shape[1]
    first = min(size, 16)
    row_id = lax.broadcasted_iota(jnp.int32, (first, columns), 0)
    first_bits = first.bit_length() - 1
    table = parity_sign(row_id & index, first_bits).astype(bf16)
    for bit_pos in range(first_bits, size.bit_length() - 1):
        table = jnp.concatenate([table, table * bit_sign(index, bit_pos).astype(bf16)], axis=0)
    return table


def index_row(ref, start, count):
    rows = [ref[pl.ds(start + step, 1), :] for step in range(count)]
    return jnp.concatenate(rows, axis=1)


def cot_products(values, index, block):
    size = values.shape[1]
    base_size = min(size, block)
    base = sign_columns(index, base_size)
    total = None
    for part in range(size // base_size):
        table = base
        if part > 0:
            sign = parity_sign((index // base_size) & part, (size // base_size).bit_length() - 1)
            table = base * sign.astype(bf16)
        piece = jnp.dot(
            values[:, part * base_size : (part + 1) * base_size], table, preferred_element_type=f32
        )
        total = piece if total is None else total + piece
    return total


def run_count(row_count):
    return 2 if row_count == 4 else 1


def quarter_index(ref, flip, runs):
    rank = lax.axis_index("rows")
    half = (lax.axis_index("ex") & 1) ^ flip
    rows = ref.shape[0] // 4 // runs
    if runs == 1:
        return index_row(ref, ((rank & 1) * 2 + half) * rows, rows)
    starts = [((rank ^ (2 * run)) * 2 + half) * rows for run in range(runs)]
    return jnp.concatenate([index_row(ref, start, rows) for start in starts], axis=1)


def right_block(values, index, block_id, row_count):
    width = values.shape[1]
    row_bits = row_count.bit_length() - 1
    parts = []
    for first in range(0, index.shape[1], 512):
        group = index[:, first : first + 512]
        part = cot_products(values, group % width, 256)
        parts.append(part * parity_sign((group // width) & block_id, row_bits))
    return parts


def block_signs(sign_ref, block_id, width):
    rows = width // sign_ref.shape[1]
    return index_row(sign_ref, block_id * rows, rows).astype(bf16)


def chunk_shape(chunk, out_rows, quarter, runs):
    if runs == 1:
        return (out_rows // 2, quarter)
    return (quarter // 2, out_rows) if chunk == 0 else (out_rows, quarter // 2)


def matrix_chunk(matrix_ref, chunk, shape, runs):
    rank = lax.axis_index("rows")
    core = lax.axis_index("ex") & 1
    rows, depth = shape
    if runs == 1:
        half = (rank & 1) ^ (chunk // 2)
        first = pl.multiple_of((half * 2 + core) * depth, depth)
        return matrix_ref.at[pl.ds(chunk % 2 * rows, rows), pl.ds(first, depth)]
    if chunk == 0:
        return matrix_ref.at[
            pl.ds(pl.multiple_of(core * rows, rows), rows),
            pl.ds(pl.multiple_of(rank * depth, depth), depth),
        ]
    block = rank ^ (0, 2, 1, 3)[chunk]
    return matrix_ref.at[:, pl.ds(pl.multiple_of((block * 2 + core) * depth, depth), depth)]


def sign_kernel(hidden_in, sign_in, out_ref, hidden_ref, sign_ref, sems):
    copies = [
        pltpu.make_async_copy(hidden_in, hidden_ref, sems.at[0]),
        pltpu.make_async_copy(sign_in, sign_ref, sems.at[1]),
    ]
    for copy in copies:
        copy.start()
    for copy in copies:
        copy.wait()
    out_ref[0] = hidden_ref[...] * sign_ref[...].astype(bf16)


def own_kernel(row_count, *refs):
    (cot_in, sign_in, col_in, row_in, len_in, matrix_ref), refs = refs[:6], refs[6:]
    right_ref, near_sign_ref, table_ref, member_ref, held_ref, last_ref, col_ref, row_ref = refs[:8]
    cot_ref, sign_ref, len_ref, sems = refs[8:]
    runs = run_count(row_count)
    pairs = (
        (cot_in, cot_ref),
        (sign_in, sign_ref),
        (col_in, col_ref),
        (row_in, row_ref),
        (len_in, len_ref),
        (matrix_chunk(matrix_ref, 2, held_ref.shape, runs), held_ref),
        (half_chunk(matrix_ref, 3, 1, last_ref.shape, runs), last_ref),
    )
    copies = [pltpu.make_async_copy(*pair, sems.at[at]) for at, pair in enumerate(pairs)]
    for copy in copies:
        copy.start()
    for copy in copies[:-2]:
        copy.wait()
    rank = lax.axis_index("rows")
    width = cot_ref.shape[1]
    near_sign_ref[...] = block_signs(sign_ref, rank ^ 1, width)

    values = cot_ref[...] * block_signs(sign_ref, rank, width)
    for flip in range(2):
        first = 0
        for part in right_block(values, quarter_index(col_ref, flip, run_count(row_count)), rank, row_count):
            right_ref[flip, :, first : first + part.shape[1]] = part
            first += part.shape[1]
    tables(row_count, row_ref, len_ref, table_ref, member_ref)
    for copy in copies[-2:]:
        copy.wait()


def tables(row_count, row_ref, len_ref, table_ref, member_ref):
    width = table_ref.shape[1]
    for flip in range(2):
        table_ref[flip] = sign_columns(quarter_index(row_ref, flip, run_count(row_count)) % width, width)
    examples, tokens = member_ref.shape
    ex_rank = lax.axis_index("ex")
    ex_count = lax.axis_size("ex")
    own = examples // ex_count
    shape = (examples, examples)
    row_id = lax.broadcasted_iota(jnp.int32, shape, 0)
    example = ((row_id // own) ^ (ex_rank & ~1) ^ (ex_count - 2)) * own + row_id % own
    other = lax.broadcasted_iota(jnp.int32, shape, 1)
    counts = jnp.broadcast_to(len_ref[...], shape)
    ends = jnp.sum(jnp.where(other <= example, counts, 0), axis=1, keepdims=True)
    starts = jnp.sum(jnp.where(other < example, counts, 0), axis=1, keepdims=True)
    position = ex_rank * tokens + lax.broadcasted_iota(jnp.int32, (examples, tokens), 1)
    inside = jnp.logical_and(position >= starts, position < ends)
    member_ref[...] = inside.astype(f32).astype(bf16)


def right_kernel(row_count, cot_ref, sign_ref, col_ref, own_ref, matrix_ref, out_ref, last_ref, sem):
    runs = run_count(row_count)
    copy = pltpu.make_async_copy(half_chunk(matrix_ref, 3, 0, last_ref.shape, runs), last_ref, sem)
    copy.start()
    rank = lax.axis_index("rows")

    @pl.when(rank >= 0)
    def _():
        values = cot_ref[...] * sign_ref[...]
        for flip in range(2):
            first = 0
            for part in right_block(values, quarter_index(col_ref, flip, runs), rank ^ 1, row_count):
                columns = slice(first, first + part.shape[1])
                out_ref[flip, :, columns] = own_ref[flip, :, columns] + part
                first += part.shape[1]

    copy.wait()


def feature_kernel(flip, row_count, masks, hidden_refs, right_ref, row_ref, table_ref, member_ref, out_ref):
    rank = lax.axis_index("rows")
    row_bits = row_count.bit_length() - 1
    blocks = [ref[block] for ref in hidden_refs for block in range(ref.shape[0])]
    base = table_ref[flip]
    high = quarter_index(row_ref, flip, run_count(row_count)) // base.shape[0]
    left = None
    for first in range(0, len(masks), 4):
        table = [
            base * parity_sign(high & (rank ^ mask), row_bits).astype(bf16)
            for mask in masks[first : first + 4]
        ]
        piece = jnp.dot(
            jnp.concatenate(blocks[first : first + 4], axis=1),
            jnp.concatenate(table, axis=0),
            preferred_element_type=f32,
        )
        left = piece if left is None else left + piece
    product = left * right_ref[flip]
    high_part = product.astype(bf16)
    low_part = (product - high_part.astype(f32)).astype(bf16)
    member = member_ref[...]
    total = jnp.dot(member, high_part, preferred_element_type=f32)
    total = total + jnp.dot(member, low_part, preferred_element_type=f32)
    out_ref[...] = total.astype(out_ref.dtype)


def half_chunk(matrix_ref, chunk, half, shape, runs):
    rows, depth = shape
    return matrix_chunk(matrix_ref, chunk, (2 * rows, depth), runs).at[pl.ds(half * rows, rows), :]


def turn_kernel(late, runs, given, matrix_ref, after_ref, *refs):
    given_refs, refs = refs[:given], refs[given:]
    loaded = 2 if late else 1
    out_refs, (*turned_refs, token_ref, sems) = refs[:loaded], refs[loaded:]
    sources = [half_chunk(matrix_ref, 1, loaded - 1, out_refs[0].shape, runs)]
    if late:
        sources.append(matrix_chunk(matrix_ref, 0, out_refs[1].shape, runs))
    copies = [
        pltpu.make_async_copy(source, ref, sems.at[at])
        for at, (source, ref) in enumerate(zip(sources, out_refs))
    ]
    for copy in copies:
        copy.start()
    token_ref[...] = jnp.zeros_like(token_ref)

    @pl.when(lax.axis_index("rows") >= 0)
    def _():
        for given_ref, turned_ref in zip(given_refs, turned_refs):
            depth = turned_ref.shape[0]
            block = math.gcd(depth, 256)
            shape = (block, block)
            same = lax.broadcasted_iota(jnp.int32, shape, 0) == lax.broadcasted_iota(jnp.int32, shape, 1)
            identity = same.astype(f32).astype(bf16)
            for first in range(0, depth, block):
                turned_ref[first : first + block, :] = lax.dot_general(
                    identity,
                    given_ref[:, first : first + block],
                    contract_last,
                    preferred_element_type=f32,
                ).astype(bf16)

    for copy in copies:
        copy.wait()


def add_kernel(kept_ref, received_ref, *refs):
    total = kept_ref[...] + received_ref[...].astype(f32)
    send_ref, total_ref = refs[-2:]
    send_ref[...] = total[: send_ref.shape[0]].astype(bf16)
    total_ref[...] = total[total.shape[0] - total_ref.shape[0] :]


def low_kernel(scale, turns, *refs):
    total = None
    for turn, ref in zip(turns, refs):
        term = ref[...].astype(f32)
        if turn:
            run = term.shape[1] // 2
            term = jnp.concatenate([term[:, run:], term[:, :run]], axis=1)
        total = term if total is None else total + term
    refs[-1][...] = (total * scale).astype(bf16)


def times_transposed(low, refs):
    parts = [
        lax.dot_general(low, ref[...], contract_last, preferred_element_type=f32) for ref in refs
    ]
    return parts[0] if len(parts) == 1 else jnp.concatenate(parts, axis=1)


def own_score_kernel(runs, low_ref, lower_ref, upper_ref, last_ref, out_ref):
    low = low_ref[...]
    if runs == 1:
        out_ref[...] = times_transposed(low, (lower_ref, upper_ref, last_ref))
    else:
        run = low.shape[1] // 2
        part = jnp.dot(low[:, :run], lower_ref[...], preferred_element_type=f32)
        upper = jnp.dot(low[:, run:], upper_ref[...], preferred_element_type=f32)
        last = times_transposed(low[:, run:], (last_ref,))
        out_ref[...] = part + jnp.concatenate([upper, last], axis=1)


def near_score_kernel(runs, low_ref, lower_ref, upper_ref, last_ref, sum_ref, send_ref, keep_ref):
    low = low_ref[...]
    if runs == 1:
        part = times_transposed(low, (lower_ref, upper_ref, last_ref))
    else:
        run = low.shape[1] // 2
        part = jnp.dot(low[:, :run], lower_ref[...], preferred_element_type=f32)
        halves = [
            jnp.dot(low[:, run:], ref[...], preferred_element_type=f32) for ref in (upper_ref, last_ref)
        ]
        part = part + jnp.concatenate(halves, axis=1)
    part = part + sum_ref[...]
    own = part.shape[0] // 2
    lower = (lax.axis_index("ex") & 1) == 0
    keep_ref[...] = jnp.where(lower, part[:own], part[own:])
    send_ref[...] = jnp.where(lower, part[own:], part[:own])


def local(hidden_acts, cotangent, lengths, row_signs, col_signs, feat_row, feat_col, inverse_rows):
    row_count = lax.axis_size("rows")
    ex_count = lax.axis_size("ex")
    tokens, width = hidden_acts.shape
    model_width = col_signs.shape[0]
    feature_count = feat_row.shape[0]
    example_count = lengths.shape[0]
    quarter = feature_count // 4
    own_examples = example_count // ex_count
    norm_scale = 1.0 / math.sqrt(width * row_count * model_width)
    whole = pl.BlockSpec(memory_space=pltpu.VMEM)
    params = pltpu.CompilerParams(vmem_limit_bytes=vmem_bytes)

    anywhere = pl.BlockSpec(memory_space=pltpu.HBM)
    out_rows = inverse_rows.shape[0]

    runs = run_count(row_count)
    chunks = [pltpu.VMEM(chunk_shape(at, out_rows, quarter, runs), bf16) for at in range(4)]
    last_rows, last_depth = chunks[3].shape
    last_chunk = pltpu.VMEM((last_rows // 2, last_depth), bf16)
    table_shape = (feature_count // 128, 128)

    near_cot = swap(cotangent, "rows", 1)
    signed = pl.pallas_call(
        sign_kernel,
        out_shape=pltpu.VMEM((1, tokens, width), bf16),
        in_specs=[anywhere] * 2,
        out_specs=whole,
        scratch_shapes=[
            pltpu.VMEM((tokens, width), bf16),
            pltpu.VMEM((1, width), jnp.int32),
            pltpu.SemaphoreType.DMA((2,)),
        ],
        compiler_params=params,
    )(in_hbm(hidden_acts), in_hbm(row_signs.reshape(1, -1)))
    group = min(row_count, 4)
    masks = [0] + list(range(1, group))[::-1]
    hidden_parts = [signed] + [swap(signed, "rows", mask) for mask in masks[1:]]
    step = group
    while step < row_count:
        held = jnp.concatenate(hidden_parts, axis=0)
        hidden_parts = [held, swap(held, "rows", step)]
        masks += [mask | step for mask in masks]
        step *= 2
    parts = len(hidden_parts)

    cot_width = cotangent.shape[1]
    lanes = min(128, cot_width)
    right_shape = pltpu.VMEM((2, tokens, quarter), f32)
    right, near_signs, hidden_table, member, matrix_2, matrix_4, col_index, row_index = pl.pallas_call(
        functools.partial(own_kernel, row_count),
        out_shape=(
            right_shape,
            pltpu.VMEM((1, cot_width), bf16),
            pltpu.VMEM((2, width, quarter), bf16),
            pltpu.VMEM((example_count, tokens), bf16),
            chunks[2],
            last_chunk,
            pltpu.VMEM(table_shape, jnp.int32),
            pltpu.VMEM(table_shape, jnp.int32),
        ),
        in_specs=[anywhere] * 6,
        out_specs=(whole,) * 8,
        scratch_shapes=[
            pltpu.VMEM(cotangent.shape, bf16),
            pltpu.VMEM((model_width // lanes, lanes), jnp.int32),
            pltpu.VMEM((1, example_count), jnp.int32),
            pltpu.SemaphoreType.DMA((7,)),
        ],
        compiler_params=params,
    )(
        in_hbm(cotangent),
        in_hbm(col_signs.reshape(-1, lanes)),
        in_hbm(feat_col.reshape(-1, 128)),
        in_hbm(feat_row.reshape(-1, 128)),
        in_hbm(lengths.reshape(1, -1)),
        in_hbm(inverse_rows),
    )
    right, matrix_3 = pl.pallas_call(
        functools.partial(right_kernel, row_count),
        out_shape=(right_shape, last_chunk),
        in_specs=[whole] * 4 + [anywhere],
        out_specs=(whole, whole),
        scratch_shapes=[pltpu.SemaphoreType.DMA],
        compiler_params=params,
    )(near_cot, near_signs, col_index, right, in_hbm(inverse_rows))

    def features(flip):
        def kernel(*refs):
            feature_kernel(flip, row_count, masks, refs[:parts], *refs[parts:])

        return pl.pallas_call(
            kernel,
            out_shape=pltpu.VMEM((example_count, quarter), bf16 if flip else f32),
            in_specs=[whole] * (parts + 4),
            out_specs=whole,
            compiler_params=params,
        )(*hidden_parts, right, row_index, hidden_table, member)

    token_shape = pltpu.VMEM((8, 128), f32)

    def load_and_turn(late, after, given):
        loaded = [last_chunk] + [chunks[0]] * late
        turned = [pltpu.VMEM(values.shape[::-1], bf16) for values in given] if runs > 1 else []
        outs = pl.pallas_call(
            functools.partial(turn_kernel, late, runs, len(given)),
            out_shape=(*loaded, *turned, token_shape),
            in_specs=[anywhere] + [whole] * (1 + len(given)),
            out_specs=(whole,) * (len(loaded) + len(turned) + 1),
            scratch_shapes=[pltpu.SemaphoreType.DMA((len(loaded),))],
            compiler_params=params,
        )(in_hbm(inverse_rows), after, *given)
        return outs[: len(loaded)], outs[len(loaded) : -1] if turned else given, outs[-1]

    def add_up(kept, received, send_count, token):
        count = received.shape[0]
        return pl.pallas_call(
            add_kernel,
            out_shape=(
                pltpu.VMEM((send_count, quarter), bf16),
                pltpu.VMEM((count - send_count % count, quarter), f32),
            ),
            in_specs=[whole] * (2 + (token is not None)),
            out_specs=(whole, whole),
            compiler_params=params,
        )(kept, received, *([] if token is None else [token]))

    def features_low(terms, turns, token):
        return pl.pallas_call(
            functools.partial(low_kernel, norm_scale, turns[: len(terms)]),
            out_shape=pltpu.VMEM(terms[0].shape, bf16),
            in_specs=[whole] * (len(terms) + (token is not None)),
            out_specs=whole,
            compiler_params=params,
        )(*terms, *([] if token is None else [token]))

    ex_masks = [1 << bit for bit in range(1, ex_count.bit_length() - 1)][::-1]
    row_masks = [1 << bit for bit in range(2, row_count.bit_length() - 1)]
    received = swap(features(1), "ex", 1)
    total = features(0)
    matrix_1, token = None, None
    for axis, mask in [("ex", mask) for mask in ex_masks] + [("rows", mask) for mask in row_masks]:
        count = received.shape[0]
        send, total = add_up(total, received, count // 2 if axis == "ex" else count, token)
        token = None
        if matrix_1 is None:
            (matrix_1,), (matrix_2, matrix_4), token = load_and_turn(
                False, send, [matrix_2, matrix_4]
            )
        received = swap(send, axis, mask)
    send, total = add_up(total, received, received.shape[0], token)
    (matrix_5, matrix_0), (matrix_1, matrix_3), token = load_and_turn(
        True, send, [matrix_1, matrix_3]
    )
    others = [swap(send, "rows", mask) for mask in range(1, group)]
    turned = runs > 1
    low = features_low([total] + others[1:2], [False, turned], token)
    near_low = features_low(others[0::2][::-1], [turned, False], None)

    part = pl.pallas_call(
        functools.partial(own_score_kernel, runs),
        out_shape=pltpu.VMEM((2 * own_examples, out_rows), f32),
        in_specs=[whole] * 4,
        out_specs=whole,
        compiler_params=params,
    )(low, matrix_0, matrix_1, matrix_5)
    own_shape = pltpu.VMEM((own_examples, out_rows), f32)
    send, keep = pl.pallas_call(
        functools.partial(near_score_kernel, runs),
        out_shape=(own_shape, own_shape),
        in_specs=[whole] * 5,
        out_specs=(whole, whole),
        compiler_params=params,
    )(near_low, matrix_2, matrix_3, matrix_4, part)
    return (keep + swap(send, "ex", 1)).astype(bf16)


def solution(mesh):
    placed = (
        P(("parts", "ex"), "rows"),
        P(("parts", "ex"), "rows"),
        P("parts"),
        P("rows"),
        P(),
        P(),
        P(),
        P("rows", None),
    )
    return jax.shard_map(
        local, mesh=mesh, in_specs=placed, out_specs=P(("parts", "ex"), "rows"), check_vma=False
    )
```
